256 devices in a mesh: slab: 64 (over y_lo, z, x), group: 4 (over y_hi, core).
Axes of the slice: x: 4, y: 4 (y_hi: 2, y_lo: 2; y = y_hi * 2 + y_lo), z: 8, core: 2. Of those that a mesh axis runs over, the one named last changes fastest.
Arguments:
- field_in: bfloat16 [4, 128, 16, 256, 256], P('group', 'slab'), may hold values from -6 to 6
- cotangent: bfloat16 [4, 128, 16, 256, 256], P('group', 'slab'), may hold values from -16 to 16
- weights: bfloat16 [2, 1024, 17, 256], P(None, 'slab'), may hold values from -1.5 to 1.5
Outputs:
- field_grad: bfloat16 [4, 128, 16, 256, 256], P('group', 'slab')
- weight_grad: float32 [2, 1024, 17, 256], P(None, ('slab', 'group'))
The draws below stay inside these ranges and needn't reach their ends.
All inputs are finite; a program needn't handle non-finite values.
Results may differ from the reference program's by a relative error of at most 0.0042.
Values sent between devices are 32-bit elements; how exact they have to be, the bound alone decides.
No kernel may reach another device: no remote copies, remote signals or barrier semaphores. Data moves between devices by JAX's collectives and lax.ppermute only.
A program may use at most 128 MiB of HBM per device.

```python
import math
import jax
import jax.numpy as jnp
from jax import lax

C = 16
NX = 256
NY = 256
KX = 32
KY = 32
KZ = 17
NZ = 128
SAMPLES = 4


def level_of(own_key, extent, cuts, low, top_value):
    factor_of = 1.0
    for dim, shards_of in cuts:
        heights = jax.random.uniform(jax.random.fold_in(jax.random.fold_in(own_key, 6), dim), (shards_of,), jnp.float32, low / len(cuts), top_value / len(cuts))
        factor_of = factor_of * jnp.repeat(jnp.exp(heights), extent[dim] // shards_of).reshape((-1,) + (1,) * (len(extent) - 1 - dim))
    return factor_of


def bell_draw(rng, shape, deviation, reach, pieces=(), kind=jnp.bfloat16):
    result = jax.random.normal(rng, shape, jnp.float32) * deviation
    if len(pieces) > 0:
        result = level_of(rng, shape, pieces, -0.22, 0.18) * result
    return jnp.clip(result, min=-reach, max=reach).astype(kind)


def setup_inputs(seed: int = 0) -> dict:
    key_list = jax.random.split(jax.random.key(seed), 4)
    return {
        "field_in": bell_draw(key_list[0], (SAMPLES, NZ, C, NX, NY), 1.0, 6.0, ((0, 4), (1, 64))),
        "cotangent": bell_draw(key_list[1], (SAMPLES, NZ, C, NX, NY), 3.0, 16.0, ((0, 4), (1, 64))),
        "weights": bell_draw(key_list[2], (2, KX * KY, KZ, C * C), C ** -0.5, 1.5, ((1, 64),)),
    }


precise = lax.Precision.HIGHEST

def kept_freqs(keep, length):
    index = jnp.arange(keep, dtype=jnp.int32)
    return jnp.where(index < keep // 2, index, length - keep + index)

def phases(positions, freqs, length):
    turns = positions[:, None] * freqs[None, :] % length
    return turns.astype(jnp.float32) * (2.0 * math.pi / length)

def plane_spectra(field):
    depth, chans, x_len, y_len = field.shape
    y_angle = phases(jnp.arange(y_len, dtype=jnp.int32), kept_freqs(KY, y_len), y_len)
    y_table = jnp.concatenate([jnp.cos(y_angle), -jnp.sin(y_angle)], 1).astype(jnp.bfloat16)
    partial_rows = jnp.einsum('zcxy,yk->zckx', field.astype(jnp.float32), y_table.astype(jnp.float32), precision=precise)
    partial_rows = partial_rows.reshape(depth, chans, 2, KY, x_len)
    x_angle = phases(jnp.arange(x_len, dtype=jnp.int32), kept_freqs(KX, x_len), x_len)
    x_table = jnp.concatenate([jnp.cos(x_angle), jnp.sin(x_angle)], 1)
    mixed = jnp.einsum('zcpkx,xq->zcpqk', partial_rows, x_table, precision=precise)
    cos_terms = mixed[:, :, :, :KX]
    sin_terms = mixed[:, :, :, KX:]
    real_part = cos_terms[:, :, 0] + sin_terms[:, :, 1]
    imag_part = cos_terms[:, :, 1] - sin_terms[:, :, 0]
    return jnp.stack([real_part, imag_part], 1).reshape(depth, 2, chans, KX * KY)

def depth_forward(spectra, positions, length):
    angle = phases(positions, jnp.arange(KZ, dtype=jnp.int32), length)
    first = jnp.einsum('zfpcm,zq->mfpcq', spectra, jnp.cos(angle), precision=precise)
    second = jnp.einsum('zfpcm,zq->mfpcq', spectra, jnp.sin(angle), precision=precise)
    real_part = first[:, :, 0] + second[:, :, 1]
    imag_part = first[:, :, 1] - second[:, :, 0]
    return jnp.stack([real_part, imag_part], 2)

def outer_modes(left, right):
    return jnp.einsum('mcq,mdq->mqcd', left, right, precision=precise)

def weight_terms(modes):
    u_real, u_imag = (modes[:, 0, 0], modes[:, 0, 1])
    g_real, g_imag = (modes[:, 1, 0], modes[:, 1, 1])
    real_part = outer_modes(u_real, g_real) + outer_modes(u_imag, g_imag)
    imag_part = outer_modes(u_real, g_imag) - outer_modes(u_imag, g_real)
    stacked = jnp.stack([real_part, imag_part], 0)
    return stacked.reshape(2, stacked.shape[1], stacked.shape[2], -1)

def apply_weights(grad, table):
    return jnp.einsum('mdq,mqcd->mcq', grad, table, precision=precise)

def mode_products(modes, weights):
    table = weights.astype(jnp.float32).reshape(2, weights.shape[1], weights.shape[2], C, C)
    g_real, g_imag = (modes[:, 1, 0], modes[:, 1, 1])
    real_part = apply_weights(g_real, table[0]) + apply_weights(g_imag, table[1])
    imag_part = apply_weights(g_imag, table[0]) - apply_weights(g_real, table[1])
    return jnp.stack([real_part, imag_part], 1)

def depth_back(grad_modes, positions, length):
    angle = phases(positions, jnp.arange(KZ, dtype=jnp.int32), length)
    first = jnp.einsum('mpcq,zq->zpcm', grad_modes, jnp.cos(angle), precision=precise)
    second = jnp.einsum('mpcq,zq->zpcm', grad_modes, jnp.sin(angle), precision=precise)
    real_part = first[:, 0] - second[:, 1]
    imag_part = second[:, 0] + first[:, 1]
    return jnp.stack([real_part, imag_part], 1)

def plane_back(planes, x_len, y_len, scale):
    depth = planes.shape[0]
    grid = planes.reshape(depth, 2, C, KX, KY)
    x_angle = phases(jnp.arange(x_len, dtype=jnp.int32), kept_freqs(KX, x_len), x_len)
    first = jnp.einsum('zpcab,xa->zpcbx', grid, jnp.cos(x_angle), precision=precise)
    second = jnp.einsum('zpcab,xa->zpcbx', grid, jnp.sin(x_angle), precision=precise)
    real_part = first[:, 0] - second[:, 1]
    imag_part = second[:, 0] + first[:, 1]
    rows = jnp.concatenate([real_part, imag_part], 2)
    y_angle = phases(jnp.arange(y_len, dtype=jnp.int32), kept_freqs(KY, y_len), y_len)
    y_table = jnp.concatenate([jnp.cos(y_angle), -jnp.sin(y_angle)], 1)
    field = jnp.einsum('zckx,yk->zcxy', rows, y_table, precision=precise)
    return (field * scale).astype(jnp.bfloat16)

def reference(field_in, cotangent, weights):
    count = field_in.shape[0]
    scale = 1.0 / math.sqrt(NX * NY * NZ)
    planes_all = jnp.arange(NZ, dtype=jnp.int32)
    grads = []
    weight_grad = jnp.zeros((2, KX * KY, KZ, C * C), jnp.float32)
    for sample in range(count):
        spectra = jnp.stack([plane_spectra(field_in[sample]), plane_spectra(cotangent[sample])], 1)
        modes = depth_forward(spectra, planes_all, NZ) * scale
        weight_grad = weight_grad + weight_terms(modes)
        grad_modes = mode_products(modes, weights)
        planes = depth_back(grad_modes, planes_all, NZ)
        grads.append(plane_back(planes, NX, NY, scale))
    return (jnp.stack(grads, 0), weight_grad)
```

```python
import math

import jax
import jax.numpy as jnp
import ml_dtypes
import numpy as np
from jax import lax
from jax.experimental import pallas as pl
from jax.experimental.pallas import tpu as pltpu
from jax.sharding import PartitionSpec as P

C = 16
KX = 32
KY = 32
KZ = 17
KP = 24
NX = 256
NY = 256
NZ = 128
SLABS = 64
HALF = KY // 2
SCALE = 1.0 / math.sqrt(NX * NY * NZ)
VMEM_LIMIT = 48 * 1024 * 1024

f32 = jnp.float32
bf16 = jnp.bfloat16


def kept_freqs(keep, length):
    index = np.arange(keep)
    return np.where(index < keep // 2, index, length - keep + index)


def phases(positions, freqs, length):
    turns = positions[:, None] * freqs[None, :] % length
    angle = turns.astype(np.float32) * np.float32(2.0 * math.pi / length)
    return angle.astype(np.float64)


def split_np(table):
    table = np.asarray(table, np.float32)
    high = table.astype(ml_dtypes.bfloat16)
    low = (table - high.astype(np.float32)).astype(ml_dtypes.bfloat16)
    return high, low


def x_forward_table():
    angle = phases(np.arange(NX), kept_freqs(KX, NX), NX)
    high, low = split_np(np.concatenate([np.cos(angle), np.sin(angle)], 1).T)
    return np.concatenate([high, low], 0)


def y_forward_table():
    angle = phases(np.arange(NY), kept_freqs(KY, NY), NY)
    real = np.cos(angle).astype(np.float32).astype(ml_dtypes.bfloat16)
    imag = (-np.sin(angle)).astype(np.float32).astype(ml_dtypes.bfloat16)
    parts = []
    for first, second in ((real, imag), (imag, -real)):
        lanes = []
        for half in range(2):
            for part in (first, second):
                cut = part[:, half * HALF:(half + 1) * HALF]
                lanes.extend([cut] * 4)
        parts.append(np.concatenate(lanes, 1))
    return np.concatenate(parts, 0)


def depth_positions():
    s = np.arange(SLABS)
    return np.concatenate([2 * s, 2 * s + 1])


def depth_forward_table():
    angle = phases(depth_positions(), np.arange(KZ), NZ)
    table = np.zeros((2 * KP, NZ), np.float32)
    table[:KZ] = np.cos(angle).T
    table[KP:KP + KZ] = np.sin(angle).T
    high, low = split_np(table)
    return np.concatenate([high, high, low], 1)


def depth_back_table():
    angle = phases(depth_positions(), np.arange(KZ), NZ)
    table = np.zeros((NZ, 2 * KP), np.float32)
    table[:, :KZ] = np.cos(angle)
    table[:, KP:KP + KZ] = np.sin(angle)
    high, low = split_np(table)
    return np.concatenate([high, high, low], 1)


def lane_fields():
    lane = np.arange(512)
    return lane // 128, lane // 64 % 2, lane // 16 % 4, lane % 16


def expand_table(which):
    cg, ri, c4, _ = lane_fields()
    col = np.arange(512)
    col_ri, ci, co = col // 256, col // 16 % 16, col % 16
    target = ci if which == 0 else co
    hit = (ri[:, None] == col_ri[None]) & ((cg * 4 + c4)[:, None] == target[None])
    return hit.astype(ml_dtypes.bfloat16)


def collect_table():
    return np.ascontiguousarray(expand_table(0).T)


def y_back_table():
    angle = phases(kept_freqs(KY, NY), np.arange(NY), NY)
    cos, sin = np.cos(angle), np.sin(angle)
    rows = []
    for half in range(2):
        cut = slice(half * HALF, (half + 1) * HALF)
        rows.extend([np.concatenate([cos[cut], sin[cut]], 1)] * 4)
        rows.extend([np.concatenate([-sin[cut], cos[cut]], 1)] * 4)
    high, low = split_np(np.concatenate(rows, 0))
    return np.concatenate([high, high, low], 0)


def x_back_table():
    angle = phases(np.arange(NX), kept_freqs(KX, NX), NX)
    table = np.concatenate([np.cos(angle), -np.sin(angle)], 1) * SCALE
    high, low = split_np(table)
    return np.concatenate([high, high, low], 1)


def dot(left, right):
    return jnp.dot(left, right, preferred_element_type=f32)


def split(value):
    high = value.astype(bf16)
    low = (value - high.astype(f32)).astype(bf16)
    return high, low


def lane_iota(rows, lanes):
    return lax.broadcasted_iota(jnp.int32, (rows, lanes), 1)


def swap_parts(value):
    tiles = [pltpu.roll(value[:, t * 128:(t + 1) * 128], 64, 1) for t in range(value.shape[1] // 128)]
    return jnp.concatenate(tiles, 1)


def forward_kernel(cot_ref, fld_ref, tx_ref, base_ref, out_ref, v_ref, tm_ref):
    step = pl.program_id(0)
    group = step % 8

    @pl.when(step == 0)
    def _():
        slot = lane_iota(256, 256) // 16 % 4
        for part in range(2):
            base = base_ref[part * 256:(part + 1) * 256, :].astype(f32)
            for c4 in range(4):
                row = (c4 * 2 + part) * 256
                tm_ref[row:row + 256, :] = jnp.where(slot == c4, base, 0.0).astype(bf16)

    def block(ref):
        row = pl.multiple_of(group * 32, 32)
        for c4 in range(4):
            mixed = dot(tx_ref[...], ref[0, 0, c4])
            high, low = split(mixed[:64] + mixed[64:])
            for part in range(2):
                lanes = slice((c4 * 2 + part) * 256, (c4 * 2 + part + 1) * 256)
                v_ref[pl.ds(row, 32), lanes] = high[part * 32:(part + 1) * 32]
                v_ref[pl.ds(row + 256, 32), lanes] = low[part * 32:(part + 1) * 32]

    @pl.when(step < 8)
    def _():
        block(cot_ref)

    @pl.when(step >= 8)
    def _():
        block(fld_ref)

    @pl.when(group == 7)
    def _():
        total = dot(v_ref[...], tm_ref[...])
        total = total[:256] + total[256:]
        first = (step // 8) * 8
        for pg in range(8):
            for half in range(2):
                piece = total[pg * 32:(pg + 1) * 32, half * 128:(half + 1) * 128]
                out_ref[pl.ds(first + half * 16 + pg, 32, stride=32), :] = piece


def forward(cotangent, field_in):
    def cot_map(i):
        j = jnp.minimum(i, 7)
        return (0, j // 4, j % 4, 0, 0)

    def fld_map(i):
        j = jnp.maximum(i - 8, 0)
        return (0, j // 4, j % 4, 0, 0)

    block = (1, 1, 4, NX, NY)
    return pl.pallas_call(
        forward_kernel,
        grid=(16,),
        out_shape=jax.ShapeDtypeStruct((SLABS * 16, 128), f32),
        in_specs=[
            pl.BlockSpec(block, cot_map),
            pl.BlockSpec(block, fld_map),
            pl.BlockSpec((128, NX), lambda i: (0, 0)),
            pl.BlockSpec((512, 256), lambda i: (0, 0)),
        ],
        out_specs=pl.BlockSpec((SLABS * 16, 128), lambda i: (0, 0)),
        scratch_shapes=[pltpu.VMEM((512, 2048), bf16), pltpu.VMEM((2048, 256), bf16)],
        compiler_params=pltpu.CompilerParams(vmem_limit_bytes=VMEM_LIMIT),
        cost_estimate=pl.CostEstimate(flops=4 * 10**9, bytes_accessed=9 * 10**6, transcendentals=0),
        name="forward_planes",
    )(cotangent, field_in, jnp.asarray(x_forward_table()), jnp.asarray(y_forward_table()))


def depth_modes(r_ref, first, tz_ref):
    tiles = []
    for cg in range(4):
        rows = [r_ref[pl.ds(first + p * 4 + cg, SLABS, stride=16), :] for p in range(2)]
        tiles.append(jnp.concatenate(rows, 0))
    high, low = split(jnp.concatenate(tiles, 1))
    both = dot(tz_ref[...], jnp.concatenate([high, low, high], 0))
    cos_part, sin_part = both[:KP], both[KP:]
    sign = jnp.where(lane_iota(KP, 512) % 128 < 64, SCALE, -SCALE)
    return cos_part * SCALE + sign * swap_parts(sin_part)


def spread(values, masks, table):
    rows = jnp.concatenate([jnp.where(mask, value, 0.0) for value, mask in zip(values, masks)], 0)
    high, low = split(rows)
    return dot(high, table) + dot(low, table)


def middle_kernel(r_ref, w_ref, tz_ref, e_ref, c_ref, tb_ref, p_ref, g_ref, prod_ref):
    modes = depth_modes(r_ref, 0, tz_ref)
    g_ref[...] = modes
    ky = lane_iota(KP, 512) % 16
    masks = [ky == m for m in range(HALF)]
    wide = spread([modes] * HALF, masks, e_ref[...])
    prod_ref[...] = jnp.zeros_like(prod_ref)
    for m in range(HALF):
        row = m * KP
        g_real, g_imag = wide[row:row + KZ, :256], wide[row:row + KZ, 256:]
        w_real, w_imag = w_ref[0, m].astype(f32), w_ref[1, m].astype(f32)
        prod_ref[row:row + KZ, :256] = g_real * w_real + g_imag * w_imag
        prod_ref[row:row + KZ, 256:] = g_imag * w_real - g_real * w_imag
    high, low = split(prod_ref[...])
    sums = dot(high, c_ref[...]) + dot(low, c_ref[...])
    direct = jnp.where(masks[0], sums[:KP], 0.0)
    for m in range(1, HALF):
        direct = direct + jnp.where(masks[m], sums[m * KP:(m + 1) * KP], 0.0)
    sign = jnp.where(lane_iota(KP, 512) % 128 < 64, -1.0, 1.0)
    turned = sign * swap_parts(direct)
    high, low = split(jnp.concatenate([direct, turned], 0))
    planes = dot(tb_ref[...], jnp.concatenate([high, low, high], 0))
    for p in range(2):
        for cg in range(4):
            piece = planes[p * SLABS:(p + 1) * SLABS, cg * 128:(cg + 1) * 128]
            p_ref[pl.ds(p * 4 + cg, SLABS, stride=8), :] = piece


def middle(received, weights):
    return pl.pallas_call(
        middle_kernel,
        out_shape=(
            jax.ShapeDtypeStruct((SLABS * 8, 128), f32),
            jax.ShapeDtypeStruct((KP, 512), f32),
        ),
        scratch_shapes=[pltpu.VMEM((HALF * KP, 512), f32)],
        compiler_params=pltpu.CompilerParams(vmem_limit_bytes=VMEM_LIMIT),
        cost_estimate=pl.CostEstimate(flops=2 * 10**9, bytes_accessed=3 * 10**6, transcendentals=0),
        name="middle_modes",
    )(
        received,
        weights,
        jnp.asarray(depth_forward_table()),
        jnp.asarray(expand_table(1)),
        jnp.asarray(collect_table()),
        jnp.asarray(depth_back_table()),
    )


def input_kernel(r_ref, tz_ref, g_ref, out_ref):
    out_ref[:, :512] = depth_modes(r_ref, 8, tz_ref)
    out_ref[:, 512:] = g_ref[...]


def input_modes(received, grad):
    return pl.pallas_call(
        input_kernel,
        out_shape=jax.ShapeDtypeStruct((KP, 1024), f32),
        compiler_params=pltpu.CompilerParams(vmem_limit_bytes=VMEM_LIMIT),
        cost_estimate=pl.CostEstimate(flops=10**8, bytes_accessed=10**6, transcendentals=0),
        name="input_modes",
    )(received, jnp.asarray(depth_forward_table()), grad)


def weight_kernel(own_ref, a_ref, b_ref, c_ref, d_ref, eu_ref, eg_ref, out_ref):
    ky = lane_iota(KP, 512) % 16 - 4 * own_ref[0]
    masks = [ky == m for m in range(4)]
    refs = (a_ref, b_ref, c_ref, d_ref)
    u_all = spread([r[:, :512] for r in refs for _ in range(4)], masks * 4, eu_ref[...])
    g_all = spread([r[:, 512:] for r in refs for _ in range(4)], masks * 4, eg_ref[...])
    for m in range(4):
        real = jnp.zeros((KP, 256), f32)
        imag = jnp.zeros((KP, 256), f32)
        for k in range(4):
            row = (k * 4 + m) * KP
            u_real, u_imag = u_all[row:row + KP, :256], u_all[row:row + KP, 256:]
            g_real, g_imag = g_all[row:row + KP, :256], g_all[row:row + KP, 256:]
            real = real + (u_real * g_real + u_imag * g_imag)
            imag = imag + (u_real * g_imag - u_imag * g_real)
        out_ref[0, m] = real[:KZ]
        out_ref[1, m] = imag[:KZ]


def weight_terms(own, pieces):
    vmem = pl.BlockSpec(memory_space=pltpu.VMEM)
    return pl.pallas_call(
        weight_kernel,
        out_shape=jax.ShapeDtypeStruct((2, 4, KZ, C * C), f32),
        in_specs=[pl.BlockSpec(memory_space=pltpu.SMEM)] + [vmem] * 6,
        out_specs=vmem,
        compiler_params=pltpu.CompilerParams(vmem_limit_bytes=VMEM_LIMIT),
        cost_estimate=pl.CostEstimate(flops=2 * 10**9, bytes_accessed=2 * 10**6, transcendentals=0),
        name="weight_terms",
    )(own, *pieces, jnp.asarray(expand_table(0)), jnp.asarray(expand_table(1)))


def back_kernel(r_ref, ty_ref, tx_ref, out_ref, q_ref):
    step = pl.program_id(0)

    @pl.when(step == 0)
    def _():
        rows = []
        for pg in range(8):
            halves = [r_ref[pl.ds(half * 8 + pg, KX, stride=16), :] for half in range(2)]
            rows.append(jnp.concatenate(halves, 1))
        grid = jnp.concatenate(rows, 0)
        slot = lane_iota(256, 256) // 16 % 4
        for c4 in range(4):
            high, low = split(jnp.where(slot == c4, grid, 0.0))
            mixed = dot(jnp.concatenate([high, low, high], 1), ty_ref[...])
            high, low = split(mixed)
            for pg in range(8):
                for part in range(2):
                    cut = (slice(pg * 32, (pg + 1) * 32), slice(part * 256, (part + 1) * 256))
                    q_ref[pg * 4 + c4, part * 32:(part + 1) * 32, :] = high[cut]
                    q_ref[pg * 4 + c4, 64 + part * 32:64 + (part + 1) * 32, :] = low[cut]

    for c4 in range(4):
        q = q_ref[step * 4 + c4]
        field = dot(tx_ref[...], jnp.concatenate([q, q[:64]], 0))
        out_ref[0, 0, c4] = field.astype(bf16)


def back(received):
    return pl.pallas_call(
        back_kernel,
        grid=(8,),
        out_shape=jax.ShapeDtypeStruct((1, 2, C, NX, NY), bf16),
        in_specs=[
            pl.BlockSpec((SLABS * 8, 128), lambda i: (0, 0)),
            pl.BlockSpec((768, 512), lambda i: (0, 0)),
            pl.BlockSpec((NX, 192), lambda i: (0, 0)),
        ],
        out_specs=pl.BlockSpec((1, 1, 4, NX, NY), lambda i: (0, i // 4, i % 4, 0, 0)),
        scratch_shapes=[pltpu.VMEM((32, 128, 256), bf16)],
        compiler_params=pltpu.CompilerParams(vmem_limit_bytes=VMEM_LIMIT),
        cost_estimate=pl.CostEstimate(flops=4 * 10**9, bytes_accessed=6 * 10**6, transcendentals=0),
        name="back_planes",
    )(received, jnp.asarray(y_back_table()), jnp.asarray(x_back_table()))


def exchange(chunks, rows):
    moved = lax.all_to_all(chunks.reshape(SLABS, rows, 128), "slab", 0, 0, tiled=True)
    return moved.reshape(SLABS * rows, 128)


def body(field_in, cotangent, weights):
    received = exchange(forward(cotangent, field_in), 16)
    planes, grad = middle(received, weights)
    returned = exchange(planes, 8)
    own = input_modes(received, grad)
    pieces = [own]
    for k in range(1, 4):
        pieces.append(lax.ppermute(own, "group", [(i, i ^ k) for i in range(4)]))
    index = lax.axis_index("group").astype(jnp.int32).reshape(1)
    weight_grad = weight_terms(index, pieces)
    return (back(returned), weight_grad)


def solution(mesh):
    in_specs = (
        P("group", "slab", None, None, None),
        P("group", "slab", None, None, None),
        P(None, "slab", None, None),
    )
    out_specs = (P("group", "slab", None, None, None), P(None, ("slab", "group"), None, None))
    return jax.shard_map(body, mesh=mesh, in_specs=in_specs, out_specs=out_specs, check_vma=False)
```

```python
import math

import jax
import jax.numpy as jnp
import ml_dtypes
import numpy as np
from jax import lax
from jax.experimental import pallas as pl
from jax.experimental.pallas import tpu as pltpu
from jax.sharding import PartitionSpec as P

C = 16
KX = 32
KY = 32
KZ = 17
KP = 24
NX = 256
NY = 256
NZ = 128
SLABS = 64
HALF = KY // 2
SCALE = 1.0 / math.sqrt(NX * NY * NZ)
VMEM_LIMIT = 48 * 1024 * 1024

f32 = jnp.float32
bf16 = jnp.bfloat16


def kept_freqs(keep, length):
    index = np.arange(keep)
    return np.where(index < keep // 2, index, length - keep + index)


def phases(positions, freqs, length):
    turns = positions[:, None] * freqs[None, :] % length
    angle = turns.astype(np.float32) * np.float32(2.0 * math.pi / length)
    return angle.astype(np.float64)


def split_np(table):
    table = np.asarray(table, np.float32)
    high = table.astype(ml_dtypes.bfloat16)
    low = (table - high.astype(np.float32)).astype(ml_dtypes.bfloat16)
    return high, low


def x_forward_table():
    angle = phases(np.arange(NX), kept_freqs(KX, NX), NX)
    high, low = split_np(np.concatenate([np.cos(angle), np.sin(angle)], 1).T)
    return np.concatenate([high, low], 0)


def y_forward_table():
    angle = phases(np.arange(NY), kept_freqs(KY, NY), NY)
    real = np.cos(angle).astype(np.float32).astype(ml_dtypes.bfloat16)
    imag = (-np.sin(angle)).astype(np.float32).astype(ml_dtypes.bfloat16)
    lanes = []
    for half in range(2):
        for part in (real, imag):
            lanes.extend([part[:, half * HALF:(half + 1) * HALF]] * 4)
    return np.concatenate(lanes, 1)


def depth_positions():
    s = np.arange(SLABS)
    return np.concatenate([2 * s, 2 * s + 1])


def depth_forward_table():
    angle = phases(depth_positions(), np.arange(KZ), NZ)
    table = np.zeros((2 * KP, NZ), np.float32)
    table[:KZ] = np.cos(angle).T
    table[KP:KP + KZ] = np.sin(angle).T
    high, low = split_np(table)
    return np.concatenate([high, high, low], 1)


def depth_back_table():
    angle = phases(depth_positions(), np.arange(KZ), NZ)
    table = np.zeros((NZ, 2 * KP), np.float32)
    table[:, :KZ] = np.cos(angle)
    table[:, KP:KP + KZ] = np.sin(angle)
    high, low = split_np(table)
    return np.concatenate([high, high, low], 1)


def lane_fields():
    lane = np.arange(512)
    return lane // 128, lane // 64 % 2, lane // 16 % 4, lane % 16


def expand_table(which):
    cg, ri, c4, _ = lane_fields()
    col = np.arange(512)
    col_ri, ci, co = col // 256, col // 16 % 16, col % 16
    target = ci if which == 0 else co
    hit = (ri[:, None] == col_ri[None]) & ((cg * 4 + c4)[:, None] == target[None])
    return hit.astype(ml_dtypes.bfloat16)


def collect_table():
    return np.ascontiguousarray(expand_table(0).T)


def y_back_table():
    angle = phases(kept_freqs(KY, NY), np.arange(NY), NY)
    cos, sin = np.cos(angle), np.sin(angle)
    rows = []
    for half in range(2):
        cut = slice(half * HALF, (half + 1) * HALF)
        rows.extend([np.concatenate([cos[cut], sin[cut]], 1)] * 4)
        rows.extend([np.concatenate([-sin[cut], cos[cut]], 1)] * 4)
    high, low = split_np(np.concatenate(rows, 0))
    return np.concatenate([high, low], 0)


def x_back_table():
    angle = phases(np.arange(NX), kept_freqs(KX, NX), NX)
    table = np.concatenate([np.cos(angle), -np.sin(angle)], 1) * SCALE
    high, low = split_np(table)
    return np.concatenate([high, high, low], 1)


def dot(left, right):
    return jnp.dot(left, right, preferred_element_type=f32)


def split(value):
    high = value.astype(bf16)
    low = (value - high.astype(f32)).astype(bf16)
    return high, low


def lane_iota(rows, lanes):
    return lax.broadcasted_iota(jnp.int32, (rows, lanes), 1)


def swap_parts(value):
    tiles = [pltpu.roll(value[:, t * 128:(t + 1) * 128], 64, 1) for t in range(value.shape[1] // 128)]
    return jnp.concatenate(tiles, 1)


STEPS = 16
WAITS = (1, 1, 2, 4, 8)


def forward_kernel(cot_hbm, fld_hbm, tx_hbm, ty_hbm, out_ref, field_ref, tx_ref, ty_ref, rows_ref, sems):
    tables = [
        pltpu.make_async_copy(ty_hbm, ty_ref, sems.at[STEPS]),
        pltpu.make_async_copy(tx_hbm, tx_ref, sems.at[STEPS + 1]),
    ]
    blocks = []
    for i in range(STEPS):
        source = cot_hbm if i < 8 else fld_hbm
        blocks.append(pltpu.make_async_copy(source.at[pl.ds(i % 8 * 4, 4)], field_ref.at[pl.ds(i * 4, 4)], sems.at[i]))
    for copy in tables + blocks:
        copy.start()
    for copy in tables:
        copy.wait()
    slot = lane_iota(NX, 256) // 16 % 4
    sign = jnp.where(lane_iota(KX, 256) % 128 < 64, 1.0, -1.0)

    def rows_y(i):
        parts = [dot(field_ref[i * 4 + c4], ty_ref[...]) for c4 in range(4)]
        rows = jnp.where(slot == 0, parts[0], jnp.where(slot == 1, parts[1], jnp.where(slot == 2, parts[2], parts[3])))
        high, low = split(rows)
        rows_ref[i % 2, 0] = high
        rows_ref[i % 2, 1] = low

    def spectrum(i):
        mixed = dot(tx_ref[...], rows_ref[i % 2, 0])
        mixed = mixed[:64] + mixed[64:] + dot(tx_ref[:64], rows_ref[i % 2, 1])
        result = mixed[:KX] + sign * swap_parts(mixed[KX:])
        for half in range(2):
            out_ref[pl.ds(half * 16 + i, KX, stride=32), :] = result[:, half * 128:(half + 1) * 128]

    first = 0
    for count in WAITS:
        for i in range(first, first + count):
            blocks[i].wait()
        for i in range(first, first + count):
            rows_y(i)
            if i > 0:
                spectrum(i - 1)
        first += count
    spectrum(STEPS - 1)


def forward(cotangent, field_in):
    anywhere = pl.BlockSpec(memory_space=pl.ANY)
    return pl.pallas_call(
        forward_kernel,
        out_shape=jax.ShapeDtypeStruct((SLABS * 16, 128), f32),
        in_specs=[anywhere] * 4,
        scratch_shapes=[
            pltpu.VMEM((STEPS * 4, NX, NY), bf16),
            pltpu.VMEM((128, NX), bf16),
            pltpu.VMEM((NY, 256), bf16),
            pltpu.VMEM((2, 2, NX, 256), bf16),
            pltpu.SemaphoreType.DMA((STEPS + 2,)),
        ],
        compiler_params=pltpu.CompilerParams(vmem_limit_bytes=60 * 1024 * 1024),
        cost_estimate=pl.CostEstimate(flops=4 * 10**9, bytes_accessed=9 * 10**6, transcendentals=0),
        name="forward_planes",
    )(
        cotangent.reshape(2 * C, NX, NY),
        field_in.reshape(2 * C, NX, NY),
        jnp.asarray(x_forward_table()),
        jnp.asarray(y_forward_table()),
    )


def depth_modes(r_ref, first, tz_ref):
    tiles = []
    for cg in range(4):
        rows = [r_ref[pl.ds(first + p * 4 + cg, SLABS, stride=16), :] for p in range(2)]
        tiles.append(jnp.concatenate(rows, 0))
    high, low = split(jnp.concatenate(tiles, 1))
    both = dot(tz_ref[...], jnp.concatenate([high, low, high], 0))
    cos_part, sin_part = both[:KP], both[KP:]
    sign = jnp.where(lane_iota(KP, 512) % 128 < 64, SCALE, -SCALE)
    return cos_part * SCALE + sign * swap_parts(sin_part)


def spread(values, masks, table):
    rows = jnp.concatenate([jnp.where(mask, value, 0.0) for value, mask in zip(values, masks)], 0)
    high, low = split(rows)
    return dot(high, table) + dot(low, table)


def middle_kernel(r_ref, w_ref, tz_ref, e_ref, c_ref, tb_ref, p_ref, g_ref, prod_ref):
    modes = depth_modes(r_ref, 0, tz_ref)
    g_ref[...] = modes
    ky = lane_iota(KP, 512) % 16
    masks = [ky == m for m in range(HALF)]
    wide = spread([modes] * HALF, masks, e_ref[...])
    prod_ref[...] = jnp.zeros_like(prod_ref)
    for m in range(HALF):
        row = m * KP
        g_real, g_imag = wide[row:row + KZ, :256], wide[row:row + KZ, 256:]
        w_real, w_imag = w_ref[0, m].astype(f32), w_ref[1, m].astype(f32)
        prod_ref[row:row + KZ, :256] = g_real * w_real + g_imag * w_imag
        prod_ref[row:row + KZ, 256:] = g_imag * w_real - g_real * w_imag
    high, low = split(prod_ref[...])
    sums = dot(high, c_ref[...]) + dot(low, c_ref[...])
    direct = jnp.where(masks[0], sums[:KP], 0.0)
    for m in range(1, HALF):
        direct = direct + jnp.where(masks[m], sums[m * KP:(m + 1) * KP], 0.0)
    sign = jnp.where(lane_iota(KP, 512) % 128 < 64, -1.0, 1.0)
    turned = sign * swap_parts(direct)
    high, low = split(jnp.concatenate([direct, turned], 0))
    planes = dot(tb_ref[...], jnp.concatenate([high, low, high], 0))
    for p in range(2):
        for cg in range(4):
            piece = planes[p * SLABS:(p + 1) * SLABS, cg * 128:(cg + 1) * 128]
            p_ref[pl.ds(p * 4 + cg, SLABS, stride=8), :] = piece


def middle(received, weights):
    return pl.pallas_call(
        middle_kernel,
        out_shape=(
            jax.ShapeDtypeStruct((SLABS * 8, 128), f32),
            jax.ShapeDtypeStruct((KP, 512), f32),
        ),
        scratch_shapes=[pltpu.VMEM((HALF * KP, 512), f32)],
        compiler_params=pltpu.CompilerParams(vmem_limit_bytes=VMEM_LIMIT),
        cost_estimate=pl.CostEstimate(flops=2 * 10**9, bytes_accessed=3 * 10**6, transcendentals=0),
        name="middle_modes",
    )(
        received,
        weights,
        jnp.asarray(depth_forward_table()),
        jnp.asarray(expand_table(1)),
        jnp.asarray(collect_table()),
        jnp.asarray(depth_back_table()),
    )


def input_kernel(r_ref, tz_ref, g_ref, out_ref):
    out_ref[:, :512] = depth_modes(r_ref, 8, tz_ref)
    out_ref[:, 512:] = g_ref[...]


def input_modes(received, grad):
    return pl.pallas_call(
        input_kernel,
        out_shape=jax.ShapeDtypeStruct((KP, 1024), f32),
        compiler_params=pltpu.CompilerParams(vmem_limit_bytes=VMEM_LIMIT),
        cost_estimate=pl.CostEstimate(flops=10**8, bytes_accessed=10**6, transcendentals=0),
        name="input_modes",
    )(received, jnp.asarray(depth_forward_table()), grad)


def weight_kernel(own_ref, a_ref, b_ref, c_ref, d_ref, eu_ref, eg_ref, out_ref):
    ky = lane_iota(KP, 512) % 16 - 4 * own_ref[0]
    masks = [ky == m for m in range(4)]
    refs = (a_ref, b_ref, c_ref, d_ref)
    u_all = spread([r[:, :512] for r in refs for _ in range(4)], masks * 4, eu_ref[...])
    g_all = spread([r[:, 512:] for r in refs for _ in range(4)], masks * 4, eg_ref[...])
    for m in range(4):
        real = jnp.zeros((KP, 256), f32)
        imag = jnp.zeros((KP, 256), f32)
        for k in range(4):
            row = (k * 4 + m) * KP
            u_real, u_imag = u_all[row:row + KP, :256], u_all[row:row + KP, 256:]
            g_real, g_imag = g_all[row:row + KP, :256], g_all[row:row + KP, 256:]
            real = real + (u_real * g_real + u_imag * g_imag)
            imag = imag + (u_real * g_imag - u_imag * g_real)
        out_ref[0, :, m, :] = real[:KZ]
        out_ref[1, :, m, :] = imag[:KZ]


def weight_terms(own, pieces):
    vmem = pl.BlockSpec(memory_space=pltpu.VMEM)
    terms = pl.pallas_call(
        weight_kernel,
        out_shape=jax.ShapeDtypeStruct((2, KZ, 4, C * C), f32),
        in_specs=[pl.BlockSpec(memory_space=pltpu.SMEM)] + [vmem] * 6,
        out_specs=vmem,
        compiler_params=pltpu.CompilerParams(vmem_limit_bytes=VMEM_LIMIT),
        cost_estimate=pl.CostEstimate(flops=2 * 10**9, bytes_accessed=2 * 10**6, transcendentals=0),
        name="weight_terms",
    )(own, *pieces, jnp.asarray(expand_table(0)), jnp.asarray(expand_table(1)))
    return terms.transpose(0, 2, 1, 3)


def back_kernel(r_ref, ty_ref, tx_ref, out_hbm, field_ref, q_ref, sems):
    rows = []
    for pg in range(8):
        halves = [r_ref[pl.ds(half * 8 + pg, KX, stride=16), :] for half in range(2)]
        rows.append(jnp.concatenate(halves, 1))
    grid = jnp.concatenate(rows, 0)
    slot = lane_iota(256, 256) // 16 % 4

    def rows_x(c4):
        high, low = split(jnp.where(slot == c4, grid, 0.0))
        mixed = dot(jnp.concatenate([high, low], 0), ty_ref[:256])
        mixed = mixed[:256] + mixed[256:] + dot(high, ty_ref[256:])
        high, low = split(mixed)
        for pg in range(8):
            for part in range(2):
                cut = (slice(pg * 32, (pg + 1) * 32), slice(part * 256, (part + 1) * 256))
                q_ref[c4, pg, part * 32:(part + 1) * 32, :] = high[cut]
                q_ref[c4, pg, 64 + part * 32:64 + (part + 1) * 32, :] = low[cut]

    copies = []
    rows_x(0)
    for c4 in range(4):
        if c4 < 3:
            rows_x(c4 + 1)
        for pg in range(8):
            q = q_ref[c4, pg]
            field_ref[pg, c4] = dot(tx_ref[...], jnp.concatenate([q, q[:64]], 0)).astype(bf16)
            copies.append(pltpu.make_async_copy(field_ref.at[pg, c4], out_hbm.at[pg, c4], sems.at[c4 * 8 + pg]))
            copies[-1].start()
    for copy in copies:
        copy.wait()


def back(received):
    field = pl.pallas_call(
        back_kernel,
        out_shape=jax.ShapeDtypeStruct((8, 4, NX, NY), bf16),
        out_specs=pl.BlockSpec(memory_space=pl.ANY),
        scratch_shapes=[
            pltpu.VMEM((8, 4, NX, NY), bf16),
            pltpu.VMEM((4, 8, 128, NY), bf16),
            pltpu.SemaphoreType.DMA((32,)),
        ],
        compiler_params=pltpu.CompilerParams(vmem_limit_bytes=VMEM_LIMIT),
        cost_estimate=pl.CostEstimate(flops=4 * 10**9, bytes_accessed=6 * 10**6, transcendentals=0),
        name="back_planes",
    )(received, jnp.asarray(y_back_table()), jnp.asarray(x_back_table()))
    return field.reshape(1, 2, C, NX, NY)


def exchange(chunks, rows):
    moved = lax.all_to_all(chunks.reshape(SLABS, rows, 128), "slab", 0, 0, tiled=True)
    return moved.reshape(SLABS * rows, 128)


def body(field_in, cotangent, weights):
    received = exchange(forward(cotangent, field_in), 16)
    planes, grad = middle(received, weights)
    returned = exchange(planes, 8)
    own = input_modes(received, grad)
    pieces = [own]
    for k in range(1, 4):
        pieces.append(lax.ppermute(own, "group", [(i, i ^ k) for i in range(4)]))
    index = lax.axis_index("group").astype(jnp.int32).reshape(1)
    field_grad = back(returned)
    pieces, field_grad = lax.optimization_barrier((pieces, field_grad))
    return (field_grad, weight_terms(index, pieces))


def solution(mesh):
    in_specs = (
        P("group", "slab", None, None, None),
        P("group", "slab", None, None, None),
        P(None, "slab", None, None),
    )
    out_specs = (P("group", "slab", None, None, None), P(None, ("slab", "group"), None, None))
    return jax.shard_map(body, mesh=mesh, in_specs=in_specs, out_specs=out_specs, check_vma=False)
```

```python
import math

import jax
import jax.numpy as jnp
import ml_dtypes
import numpy as np
from jax import lax
from jax.experimental import pallas as pl
from jax.experimental.pallas import tpu as pltpu
from jax.sharding import PartitionSpec as P

C = 16
KX = 32
KY = 32
KZ = 17
KP = 24
NX = 256
NY = 256
NZ = 128
SLABS = 64
HALF = KY // 2
SCALE = 1.0 / math.sqrt(NX * NY * NZ)
VMEM_LIMIT = 48 * 1024 * 1024

f32 = jnp.float32
bf16 = jnp.bfloat16


def kept_freqs(keep, length):
    index = np.arange(keep)
    return np.where(index < keep // 2, index, length - keep + index)


def phases(positions, freqs, length):
    turns = positions[:, None] * freqs[None, :] % length
    angle = turns.astype(np.float32) * np.float32(2.0 * math.pi / length)
    return angle.astype(np.float64)


def split_np(table):
    table = np.asarray(table, np.float32)
    high = table.astype(ml_dtypes.bfloat16)
    low = (table - high.astype(np.float32)).astype(ml_dtypes.bfloat16)
    return high, low


def x_forward_table():
    angle = phases(np.arange(NX), kept_freqs(KX, NX), NX)
    high, low = split_np(np.concatenate([np.cos(angle), np.sin(angle)], 1).T)
    return np.concatenate([high, low], 0)


def y_forward_table():
    angle = phases(np.arange(NY), kept_freqs(KY, NY), NY)
    real = np.cos(angle).astype(np.float32).astype(ml_dtypes.bfloat16)
    imag = (-np.sin(angle)).astype(np.float32).astype(ml_dtypes.bfloat16)
    lanes = []
    for half in range(2):
        for part in (real, imag):
            lanes.extend([part[:, half * HALF:(half + 1) * HALF]] * 4)
    return np.concatenate(lanes, 1)


def depth_positions():
    s = np.arange(SLABS)
    return np.concatenate([2 * s, 2 * s + 1])


def depth_forward_table():
    angle = phases(depth_positions(), np.arange(KZ), NZ)
    table = np.zeros((2 * KP, NZ), np.float32)
    table[:KZ] = np.cos(angle).T
    table[KP:KP + KZ] = np.sin(angle).T
    high, low = split_np(table)
    return np.concatenate([high, high, low], 1)


def depth_back_table():
    angle = phases(depth_positions(), np.arange(KZ), NZ)
    table = np.zeros((NZ, 2 * KP), np.float32)
    table[:, :KZ] = np.cos(angle)
    table[:, KP:KP + KZ] = np.sin(angle)
    high, low = split_np(table)
    return np.concatenate([high, high, low], 1)


def channel_mode_lanes():
    lane = np.arange(256)
    return lane // 16, lane % 16


def expand_table():
    c, _ = channel_mode_lanes()
    col = np.arange(256)
    return (c[:, None] == (col % 16)[None]).astype(ml_dtypes.bfloat16)


def collect_table():
    c, _ = channel_mode_lanes()
    row = np.arange(256)
    return ((row // 16)[:, None] == c[None]).astype(ml_dtypes.bfloat16)


def quarter_table():
    c, ky = channel_mode_lanes()
    table = np.zeros((2, 256, 512), np.float32)
    for part in range(2):
        table[part, np.arange(256), ky // 4 * 128 + part * 64 + c * 4 + ky % 4] = 1.0
    return table.reshape(512, 512).astype(ml_dtypes.bfloat16)


def owned_table(which):
    row, col = np.arange(128), np.arange(512)
    target = col // 16 % 16 if which == 0 else col % 16
    hit = (row // 64)[:, None] == (col // 256)[None]
    return (hit & ((row // 4 % 16)[:, None] == target[None])).astype(ml_dtypes.bfloat16)


def y_back_table():
    angle = phases(kept_freqs(KY, NY), np.arange(NY), NY)
    cos, sin = np.cos(angle), np.sin(angle)
    rows = []
    for half in range(2):
        cut = slice(half * HALF, (half + 1) * HALF)
        rows.extend([np.concatenate([cos[cut], sin[cut]], 1)] * 4)
        rows.extend([np.concatenate([-sin[cut], cos[cut]], 1)] * 4)
    high, low = split_np(np.concatenate(rows, 0))
    return np.concatenate([high, low], 0)


def x_back_table():
    angle = phases(np.arange(NX), kept_freqs(KX, NX), NX)
    table = np.concatenate([np.cos(angle), -np.sin(angle)], 1) * SCALE
    high, low = split_np(table)
    return np.concatenate([high, high, low], 1)


def dot(left, right):
    return jnp.dot(left, right, preferred_element_type=f32)


def split(value):
    high = value.astype(bf16)
    low = (value - high.astype(f32)).astype(bf16)
    return high, low


def lane_iota(rows, lanes):
    return lax.broadcasted_iota(jnp.int32, (rows, lanes), 1)


def swap_parts(value):
    tiles = [pltpu.roll(value[:, t * 128:(t + 1) * 128], 64, 1) for t in range(value.shape[1] // 128)]
    return jnp.concatenate(tiles, 1)


STEPS = 16
WAITS = (1, 1, 2, 4, 8)


def forward_kernel(cot_hbm, fld_hbm, tx_hbm, ty_hbm, out_ref, field_ref, tx_ref, ty_ref, rows_ref, sems):
    tables = [
        pltpu.make_async_copy(ty_hbm, ty_ref, sems.at[STEPS]),
        pltpu.make_async_copy(tx_hbm, tx_ref, sems.at[STEPS + 1]),
    ]
    blocks = []
    for i in range(STEPS):
        source = cot_hbm if i < 8 else fld_hbm
        blocks.append(pltpu.make_async_copy(source.at[pl.ds(i % 8 * 4, 4)], field_ref.at[pl.ds(i * 4, 4)], sems.at[i]))
    for copy in tables + blocks:
        copy.start()
    for copy in tables:
        copy.wait()
    slot = lane_iota(NX, 256) // 16 % 4
    sign = jnp.where(lane_iota(KX, 256) % 128 < 64, 1.0, -1.0)

    def rows_y(i):
        parts = [dot(field_ref[i * 4 + c4], ty_ref[...]) for c4 in range(4)]
        rows = jnp.where(slot == 0, parts[0], jnp.where(slot == 1, parts[1], jnp.where(slot == 2, parts[2], parts[3])))
        high, low = split(rows)
        rows_ref[i % 2, 0] = high
        rows_ref[i % 2, 1] = low

    def spectrum(i):
        mixed = dot(tx_ref[...], rows_ref[i % 2, 0])
        mixed = mixed[:64] + mixed[64:] + dot(tx_ref[:64], rows_ref[i % 2, 1])
        result = mixed[:KX] + sign * swap_parts(mixed[KX:])
        for half in range(2):
            out_ref[pl.ds(half * 16 + i, KX, stride=32), :] = result[:, half * 128:(half + 1) * 128]

    first = 0
    for count in WAITS:
        for i in range(first, first + count):
            blocks[i].wait()
        for i in range(first, first + count):
            rows_y(i)
            if i > 0:
                spectrum(i - 1)
        first += count
    spectrum(STEPS - 1)


def forward(cotangent, field_in):
    anywhere = pl.BlockSpec(memory_space=pl.ANY)
    return pl.pallas_call(
        forward_kernel,
        out_shape=jax.ShapeDtypeStruct((SLABS * 16, 128), f32),
        in_specs=[anywhere] * 4,
        scratch_shapes=[
            pltpu.VMEM((STEPS * 4, NX, NY), bf16),
            pltpu.VMEM((128, NX), bf16),
            pltpu.VMEM((NY, 256), bf16),
            pltpu.VMEM((2, 2, NX, 256), bf16),
            pltpu.SemaphoreType.DMA((STEPS + 2,)),
        ],
        compiler_params=pltpu.CompilerParams(vmem_limit_bytes=60 * 1024 * 1024),
        cost_estimate=pl.CostEstimate(flops=4 * 10**9, bytes_accessed=9 * 10**6, transcendentals=0),
        name="forward_planes",
    )(
        cotangent.reshape(2 * C, NX, NY),
        field_in.reshape(2 * C, NX, NY),
        jnp.asarray(x_forward_table()),
        jnp.asarray(y_forward_table()),
    )


def roll_half(value):
    return pltpu.roll(value, 64, 1)


def depth_modes(r_ref, first, tz_ref):
    tiles = []
    for cg in range(4):
        rows = [r_ref[pl.ds(first + p * 4 + cg, SLABS, stride=16), :] for p in range(2)]
        tiles.append(jnp.concatenate(rows, 0))
    high, low = split(jnp.concatenate(tiles, 1))
    both = dot(tz_ref[...], jnp.concatenate([high, low, high], 0)) * SCALE
    left = lane_iota(KP, 128) < 64
    real, imag = [], []
    for pair in range(2):
        cuts = [slice((2 * pair + j) * 128, (2 * pair + j + 1) * 128) for j in range(2)]
        c0, c1 = both[:KP, cuts[0]], both[:KP, cuts[1]]
        s0, s1 = both[KP:, cuts[0]], both[KP:, cuts[1]]
        real.append(jnp.where(left, c0 + roll_half(s0), roll_half(c1) + s1))
        imag.append(jnp.where(left, roll_half(c0) - s0, c1 - roll_half(s1)))
    return jnp.concatenate(real, 1), jnp.concatenate(imag, 1)


def precise_dot(value, table):
    high, low = split(value)
    both = dot(jnp.concatenate([high, low], 0), table)
    return both[:value.shape[0]] + both[value.shape[0]:]


def middle_kernel(r_ref, w_ref, tz_ref, e_ref, c_ref, tb_ref, p_ref, g_ref, sum_ref):
    g_real, g_imag = depth_modes(r_ref, 0, tz_ref)
    g_ref[:KP] = g_real
    g_ref[KP:] = g_imag
    own = lane_iota(HALF, 256) % 16 == lax.broadcasted_iota(jnp.int32, (HALF, 256), 0)
    rows = []
    for part in range(2):
        for kz in range(KZ):
            line = g_ref[part * KP + kz:part * KP + kz + 1, :]
            rows.append(jnp.where(own, jnp.broadcast_to(line, (HALF, 256)), 0.0))
    wide = precise_dot(jnp.concatenate(rows, 0), e_ref[...])
    real, imag = [], []
    for kz in range(KZ):
        g_r = wide[kz * HALF:(kz + 1) * HALF]
        g_i = wide[(KZ + kz) * HALF:(KZ + kz + 1) * HALF]
        w_r, w_i = w_ref[0, kz].astype(f32), w_ref[1, kz].astype(f32)
        real.append(g_r * w_r + g_i * w_i)
        imag.append(g_i * w_r - g_r * w_i)
    sums = precise_dot(jnp.concatenate(real + imag, 0), c_ref[...])
    sum_ref[...] = jnp.zeros_like(sum_ref)
    for part in range(2):
        for kz in range(KZ):
            row = (part * KZ + kz) * HALF
            kept = jnp.where(own, sums[row:row + HALF], 0.0)
            sum_ref[part * KP + kz:part * KP + kz + 1, :] = jnp.sum(kept, axis=0, keepdims=True)
    left = lane_iota(KP, 128) < 64
    direct, turned = [], []
    for pair in range(2):
        cut = slice(pair * 128, (pair + 1) * 128)
        re, im = sum_ref[:KP, cut], sum_ref[KP:, cut]
        re_roll, im_roll = roll_half(re), roll_half(im)
        direct.extend([jnp.where(left, re, im_roll), jnp.where(left, re_roll, im)])
        turned.extend([jnp.where(left, -im, re_roll), jnp.where(left, -im_roll, re)])
    stacked = jnp.concatenate([jnp.concatenate(direct, 1), jnp.concatenate(turned, 1)], 0)
    high, low = split(stacked)
    planes = dot(tb_ref[...], jnp.concatenate([high, low, high], 0))
    for p in range(2):
        for cg in range(4):
            piece = planes[p * SLABS:(p + 1) * SLABS, cg * 128:(cg + 1) * 128]
            p_ref[pl.ds(p * 4 + cg, SLABS, stride=8), :] = piece


def middle(received, weights):
    return pl.pallas_call(
        middle_kernel,
        out_shape=(
            jax.ShapeDtypeStruct((SLABS * 8, 128), f32),
            jax.ShapeDtypeStruct((2 * KP, 256), f32),
        ),
        scratch_shapes=[pltpu.VMEM((2 * KP, 256), f32)],
        compiler_params=pltpu.CompilerParams(vmem_limit_bytes=VMEM_LIMIT),
        cost_estimate=pl.CostEstimate(flops=2 * 10**9, bytes_accessed=3 * 10**6, transcendentals=0),
        name="middle_modes",
    )(
        received,
        weights.transpose(0, 2, 1, 3),
        jnp.asarray(depth_forward_table()),
        jnp.asarray(expand_table()),
        jnp.asarray(collect_table()),
        jnp.asarray(depth_back_table()),
    )


def input_kernel(index_ref, r_ref, tz_ref, g_ref, cut_ref, own_ref, first_ref, second_ref, third_ref, all_ref):
    u_real, u_imag = depth_modes(r_ref, 8, tz_ref)
    real = jnp.concatenate([u_real, g_ref[:KP]], 0)
    imag = jnp.concatenate([u_imag, g_ref[KP:]], 0)
    lanes = precise_dot(real, cut_ref[:256]) + precise_dot(imag, cut_ref[256:])
    for owner in range(4):
        for field in range(2):
            piece = lanes[field * KP:(field + 1) * KP, owner * 128:(owner + 1) * 128]
            all_ref[owner, :, field * 128:(field + 1) * 128] = piece
    me = index_ref[0]
    for k, ref in enumerate((own_ref, first_ref, second_ref, third_ref)):
        ref[...] = all_ref[me ^ k]


def input_modes(index, received, grad):
    vmem = pl.BlockSpec(memory_space=pltpu.VMEM)
    return pl.pallas_call(
        input_kernel,
        out_shape=(jax.ShapeDtypeStruct((KP, 256), f32),) * 4,
        in_specs=[pl.BlockSpec(memory_space=pltpu.SMEM)] + [vmem] * 4,
        out_specs=(vmem,) * 4,
        scratch_shapes=[pltpu.VMEM((4, KP, 256), f32)],
        compiler_params=pltpu.CompilerParams(vmem_limit_bytes=VMEM_LIMIT),
        cost_estimate=pl.CostEstimate(flops=10**8, bytes_accessed=10**6, transcendentals=0),
        name="input_modes",
    )(index, received, jnp.asarray(depth_forward_table()), grad, jnp.asarray(quarter_table()))


def weight_kernel(a_ref, b_ref, c_ref, d_ref, eu_ref, eg_ref, out_ref, u_ref, g_ref):
    mode = lane_iota(KP, 128) % 4
    for k, ref in enumerate((a_ref, b_ref, c_ref, d_ref)):
        for m in range(4):
            rows = pl.ds(k * 4 * KP + m, KP, stride=4)
            u_ref[rows, :] = jnp.where(mode == m, ref[:, :128], 0.0)
            g_ref[rows, :] = jnp.where(mode == m, ref[:, 128:], 0.0)
    u_all = precise_dot(u_ref[...], eu_ref[...])
    g_all = precise_dot(g_ref[...], eg_ref[...])
    real = jnp.zeros((4 * KP, 256), f32)
    imag = jnp.zeros((4 * KP, 256), f32)
    for k in range(4):
        cut = slice(k * 4 * KP, (k + 1) * 4 * KP)
        u_r, u_i = u_all[cut, :256], u_all[cut, 256:]
        g_r, g_i = g_all[cut, :256], g_all[cut, 256:]
        real = real + (u_r * g_r + u_i * g_i)
        imag = imag + (u_r * g_i - u_i * g_r)
    for kz in range(KZ):
        out_ref[0, kz] = real[kz * 4:(kz + 1) * 4]
        out_ref[1, kz] = imag[kz * 4:(kz + 1) * 4]


def weight_terms(pieces):
    terms = pl.pallas_call(
        weight_kernel,
        out_shape=jax.ShapeDtypeStruct((2, KZ, 4, C * C), f32),
        scratch_shapes=[pltpu.VMEM((16 * KP, 128), f32), pltpu.VMEM((16 * KP, 128), f32)],
        compiler_params=pltpu.CompilerParams(vmem_limit_bytes=VMEM_LIMIT),
        cost_estimate=pl.CostEstimate(flops=2 * 10**9, bytes_accessed=2 * 10**6, transcendentals=0),
        name="weight_terms",
    )(*pieces, jnp.asarray(owned_table(0)), jnp.asarray(owned_table(1)))
    return terms.transpose(0, 2, 1, 3)


def back_kernel(r_ref, ty_ref, tx_ref, out_hbm, field_ref, q_ref, sems):
    rows = []
    for pg in range(8):
        halves = [r_ref[pl.ds(half * 8 + pg, KX, stride=16), :] for half in range(2)]
        rows.append(jnp.concatenate(halves, 1))
    grid = jnp.concatenate(rows, 0)
    slot = lane_iota(256, 256) // 16 % 4

    def rows_x(c4):
        high, low = split(jnp.where(slot == c4, grid, 0.0))
        mixed = dot(jnp.concatenate([high, low], 0), ty_ref[:256])
        mixed = mixed[:256] + mixed[256:] + dot(high, ty_ref[256:])
        high, low = split(mixed)
        for pg in range(8):
            for part in range(2):
                cut = (slice(pg * 32, (pg + 1) * 32), slice(part * 256, (part + 1) * 256))
                q_ref[c4, pg, part * 32:(part + 1) * 32, :] = high[cut]
                q_ref[c4, pg, 64 + part * 32:64 + (part + 1) * 32, :] = low[cut]

    copies = []
    rows_x(0)
    for c4 in range(4):
        if c4 < 3:
            rows_x(c4 + 1)
        for pg in range(8):
            q = q_ref[c4, pg]
            field_ref[pg, c4] = dot(tx_ref[...], jnp.concatenate([q, q[:64]], 0)).astype(bf16)
            copies.append(pltpu.make_async_copy(field_ref.at[pg, c4], out_hbm.at[pg, c4], sems.at[c4 * 8 + pg]))
            copies[-1].start()
    for copy in copies:
        copy.wait()


def back(received):
    field = pl.pallas_call(
        back_kernel,
        out_shape=jax.ShapeDtypeStruct((8, 4, NX, NY), bf16),
        out_specs=pl.BlockSpec(memory_space=pl.ANY),
        scratch_shapes=[
            pltpu.VMEM((8, 4, NX, NY), bf16),
            pltpu.VMEM((4, 8, 128, NY), bf16),
            pltpu.SemaphoreType.DMA((32,)),
        ],
        compiler_params=pltpu.CompilerParams(vmem_limit_bytes=VMEM_LIMIT),
        cost_estimate=pl.CostEstimate(flops=4 * 10**9, bytes_accessed=6 * 10**6, transcendentals=0),
        name="back_planes",
    )(received, jnp.asarray(y_back_table()), jnp.asarray(x_back_table()))
    return field.reshape(1, 2, C, NX, NY)


def exchange(chunks, rows):
    moved = lax.all_to_all(chunks.reshape(SLABS, rows, 128), "slab", 0, 0, tiled=True)
    return moved.reshape(SLABS * rows, 128)


def body(field_in, cotangent, weights):
    index = lax.axis_index("group").astype(jnp.int32).reshape(1)
    received = exchange(forward(cotangent, field_in), 16)
    planes, grad = middle(received, weights)
    returned = exchange(planes, 8)
    pieces = list(input_modes(index, received, grad))
    for k in range(1, 4):
        pieces[k] = lax.ppermute(pieces[k], "group", [(i, i ^ k) for i in range(4)])
    weight_grad = weight_terms(pieces)
    return (back(returned), weight_grad)


def solution(mesh):
    in_specs = (
        P("group", "slab", None, None, None),
        P("group", "slab", None, None, None),
        P(None, "slab", None, None),
    )
    out_specs = (P("group", "slab", None, None, None), P(None, ("slab", "group"), None, None))
    return jax.shard_map(body, mesh=mesh, in_specs=in_specs, out_specs=out_specs, check_vma=False)
```

```python
import math

import jax
import jax.numpy as jnp
import ml_dtypes
import numpy as np
from jax import lax
from jax.experimental import pallas as pl
from jax.experimental.pallas import tpu as pltpu
from jax.sharding import PartitionSpec as P

C = 16
KX = 32
KY = 32
KZ = 17
KP = 24
NX = 256
NY = 256
NZ = 128
SLABS = 64
HALF = KY // 2
SCALE = 1.0 / math.sqrt(NX * NY * NZ)
VMEM_LIMIT = 48 * 1024 * 1024

f32 = jnp.float32
bf16 = jnp.bfloat16


def kept_freqs(keep, length):
    index = np.arange(keep)
    return np.where(index < keep // 2, index, length - keep + index)


def phases(positions, freqs, length):
    turns = positions[:, None] * freqs[None, :] % length
    angle = turns.astype(np.float32) * np.float32(2.0 * math.pi / length)
    return angle.astype(np.float64)


def split_np(table):
    table = np.asarray(table, np.float32)
    high = table.astype(ml_dtypes.bfloat16)
    low = (table - high.astype(np.float32)).astype(ml_dtypes.bfloat16)
    return high, low


def x_forward_table():
    angle = phases(np.arange(NX), kept_freqs(KX, NX), NX)
    high, low = split_np(np.concatenate([np.cos(angle), np.sin(angle)], 1).T)
    return np.concatenate([high, low], 0)


def y_forward_table():
    angle = phases(np.arange(NY), kept_freqs(KY, NY), NY)
    real = np.cos(angle).astype(np.float32).astype(ml_dtypes.bfloat16)
    imag = (-np.sin(angle)).astype(np.float32).astype(ml_dtypes.bfloat16)
    lanes = []
    for half in range(2):
        for part in (real, imag):
            lanes.extend([part[:, half * HALF:(half + 1) * HALF]] * 4)
    return np.concatenate(lanes, 1)


def depth_positions():
    s = np.arange(SLABS)
    return np.concatenate([2 * s, 2 * s + 1])


def depth_forward_table():
    angle = phases(depth_positions(), np.arange(KZ), NZ)
    table = np.zeros((2 * KP, NZ), np.float32)
    table[:KZ] = np.cos(angle).T
    table[KP:KP + KZ] = np.sin(angle).T
    high, low = split_np(table)
    return np.concatenate([high, high, low], 1)


def depth_back_table():
    angle = phases(depth_positions(), np.arange(KZ), NZ)
    table = np.zeros((NZ, 2 * KP), np.float32)
    table[:, :KZ] = np.cos(angle)
    table[:, KP:KP + KZ] = np.sin(angle)
    high, low = split_np(table)
    return np.concatenate([high, high, low], 1)


def channel_mode_lanes():
    lane = np.arange(256)
    return lane // 16, lane % 16


def expand_table():
    c, _ = channel_mode_lanes()
    col = np.arange(256)
    return (c[:, None] == (col % 16)[None]).astype(ml_dtypes.bfloat16)


def collect_table():
    row, col = np.arange(512), np.arange(512)
    channel = col // 128 * 4 + col // 32 % 4
    hit = (row // 256)[:, None] == (col // 16 % 2)[None]
    return (hit & ((row // 16 % 16)[:, None] == channel[None])).astype(ml_dtypes.bfloat16)


def quarter_table():
    c, ky = channel_mode_lanes()
    table = np.zeros((2, 256, 512), np.float32)
    for part in range(2):
        table[part, np.arange(256), ky // 4 * 128 + part * 64 + c * 4 + ky % 4] = 1.0
    return table.reshape(512, 512).astype(ml_dtypes.bfloat16)


def owned_table(which):
    row, col = np.arange(128), np.arange(512)
    target = col // 16 % 16 if which == 0 else col % 16
    hit = (row // 64)[:, None] == (col // 256)[None]
    return (hit & ((row // 4 % 16)[:, None] == target[None])).astype(ml_dtypes.bfloat16)


def y_back_table():
    angle = phases(kept_freqs(KY, NY), np.arange(NY), NY)
    cos, sin = np.cos(angle), np.sin(angle)
    rows = []
    for half in range(2):
        cut = slice(half * HALF, (half + 1) * HALF)
        rows.append(np.concatenate([cos[cut], sin[cut]], 1))
        rows.append(np.concatenate([-sin[cut], cos[cut]], 1))
    high, low = split_np(np.concatenate(rows, 0))
    return np.concatenate([high, high, low, np.zeros_like(low)], 0)


def x_back_table():
    angle = phases(np.arange(NX), kept_freqs(KX, NX), NX)
    table = np.concatenate([np.cos(angle), -np.sin(angle)], 1) * SCALE
    high, low = split_np(table)
    return np.concatenate([high, high, low], 1)


def dot(left, right):
    return jnp.dot(left, right, preferred_element_type=f32)


def split(value):
    high = value.astype(bf16)
    low = (value - high.astype(f32)).astype(bf16)
    return high, low


def lane_iota(rows, lanes):
    return lax.broadcasted_iota(jnp.int32, (rows, lanes), 1)


def swap_parts(value):
    tiles = [pltpu.roll(value[:, t * 128:(t + 1) * 128], 64, 1) for t in range(value.shape[1] // 128)]
    return jnp.concatenate(tiles, 1)


STEPS = 16
WAITS = (1, 1, 2, 4, 8)


def forward_kernel(cot_hbm, fld_hbm, tx_hbm, ty_hbm, out_ref, field_ref, tx_ref, ty_ref, rows_ref, sems):
    tables = [
        pltpu.make_async_copy(ty_hbm, ty_ref, sems.at[STEPS]),
        pltpu.make_async_copy(tx_hbm, tx_ref, sems.at[STEPS + 1]),
    ]
    blocks = []
    for i in range(STEPS):
        source = cot_hbm if i < 8 else fld_hbm
        blocks.append(pltpu.make_async_copy(source.at[pl.ds(i % 8 * 4, 4)], field_ref.at[pl.ds(i * 4, 4)], sems.at[i]))
    for copy in tables + blocks:
        copy.start()
    for copy in tables:
        copy.wait()
    slot = lane_iota(NX, 256) // 16 % 4
    sign = jnp.where(lane_iota(KX, 256) % 128 < 64, 1.0, -1.0)

    def rows_y(i):
        parts = [dot(field_ref[i * 4 + c4], ty_ref[...]) for c4 in range(4)]
        rows = jnp.where(slot == 0, parts[0], jnp.where(slot == 1, parts[1], jnp.where(slot == 2, parts[2], parts[3])))
        high, low = split(rows)
        rows_ref[i % 2, 0] = high
        rows_ref[i % 2, 1] = low

    def spectrum(i):
        mixed = dot(tx_ref[...], rows_ref[i % 2, 0])
        mixed = mixed[:64] + mixed[64:] + dot(tx_ref[:64], rows_ref[i % 2, 1])
        result = mixed[:KX] + sign * swap_parts(mixed[KX:])
        for half in range(2):
            out_ref[pl.ds(half * 16 + i, KX, stride=32), :] = result[:, half * 128:(half + 1) * 128]

    first = 0
    for count in WAITS:
        for i in range(first, first + count):
            blocks[i].wait()
        for i in range(first, first + count):
            rows_y(i)
            if i > 0:
                spectrum(i - 1)
        first += count
    spectrum(STEPS - 1)


def forward(cotangent, field_in):
    anywhere = pl.BlockSpec(memory_space=pl.ANY)
    return pl.pallas_call(
        forward_kernel,
        out_shape=pltpu.VMEM((SLABS * 16, 128), f32),
        in_specs=[anywhere] * 4,
        scratch_shapes=[
            pltpu.VMEM((STEPS * 4, NX, NY), bf16),
            pltpu.VMEM((128, NX), bf16),
            pltpu.VMEM((NY, 256), bf16),
            pltpu.VMEM((2, 2, NX, 256), bf16),
            pltpu.SemaphoreType.DMA((STEPS + 2,)),
        ],
        compiler_params=pltpu.CompilerParams(vmem_limit_bytes=60 * 1024 * 1024),
        cost_estimate=pl.CostEstimate(flops=4 * 10**9, bytes_accessed=9 * 10**6, transcendentals=0),
        name="forward_planes",
    )(
        cotangent.reshape(2 * C, NX, NY),
        field_in.reshape(2 * C, NX, NY),
        jnp.asarray(x_forward_table()),
        jnp.asarray(y_forward_table()),
    )


def roll_half(value):
    return pltpu.roll(value, 64, 1)


def depth_modes(r_ref, first, tz_ref):
    tiles = []
    for cg in range(4):
        rows = [r_ref[pl.ds(first + p * 4 + cg, SLABS, stride=16), :] for p in range(2)]
        tiles.append(jnp.concatenate(rows, 0))
    high, low = split(jnp.concatenate(tiles, 1))
    both = dot(tz_ref[...], jnp.concatenate([high, low, high], 0)) * SCALE
    left = lane_iota(KP, 128) < 64
    real, imag = [], []
    for pair in range(2):
        cuts = [slice((2 * pair + j) * 128, (2 * pair + j + 1) * 128) for j in range(2)]
        c0, c1 = both[:KP, cuts[0]], both[:KP, cuts[1]]
        s0, s1 = both[KP:, cuts[0]], both[KP:, cuts[1]]
        real.append(jnp.where(left, c0 + roll_half(s0), roll_half(c1) + s1))
        imag.append(jnp.where(left, roll_half(c0) - s0, c1 - roll_half(s1)))
    return jnp.concatenate(real, 1), jnp.concatenate(imag, 1)


def precise_dot(value, table):
    high, low = split(value)
    both = dot(jnp.concatenate([high, low], 0), table)
    return both[:value.shape[0]] + both[value.shape[0]:]


def middle_kernel(r_ref, w_ref, tz_ref, e_ref, c_ref, tb_ref, p_ref, g_ref, sum_ref):
    g_real, g_imag = depth_modes(r_ref, 0, tz_ref)
    g_ref[:KP] = g_real
    g_ref[KP:] = g_imag
    own = lane_iota(HALF, 256) % 16 == lax.broadcasted_iota(jnp.int32, (HALF, 256), 0)
    rows = []
    for part in range(2):
        for kz in range(KZ):
            line = g_ref[part * KP + kz:part * KP + kz + 1, :]
            rows.append(jnp.where(own, jnp.broadcast_to(line, (HALF, 256)), 0.0))
    wide = precise_dot(jnp.concatenate(rows, 0), e_ref[...])
    products = []
    for kz in range(KZ):
        g_r = wide[kz * HALF:(kz + 1) * HALF]
        g_i = wide[(KZ + kz) * HALF:(KZ + kz + 1) * HALF]
        w_r, w_i = w_ref[0, kz].astype(f32), w_ref[1, kz].astype(f32)
        products.append(jnp.concatenate([g_r * w_r + g_i * w_i, g_i * w_r - g_r * w_i], 1))
    sums = precise_dot(jnp.concatenate(products, 0), c_ref[...])
    own = jnp.concatenate([own, own], 1)
    sum_ref[...] = jnp.zeros_like(sum_ref)
    for kz in range(KZ):
        kept = jnp.where(own, sums[kz * HALF:(kz + 1) * HALF], 0.0)
        sum_ref[kz:kz + 1, :] = jnp.sum(kept, axis=0, keepdims=True)
    direct = sum_ref[...]
    real_lane = lane_iota(KP, 128) % 32 < 16
    turned = []
    for cg in range(4):
        tile = direct[:, cg * 128:(cg + 1) * 128]
        turned.append(jnp.where(real_lane, -pltpu.roll(tile, 112, 1), pltpu.roll(tile, 16, 1)))
    stacked = jnp.concatenate([direct, jnp.concatenate(turned, 1)], 0)
    high, low = split(stacked)
    planes = dot(tb_ref[...], jnp.concatenate([high, low, high], 0))
    for p in range(2):
        for cg in range(4):
            piece = planes[p * SLABS:(p + 1) * SLABS, cg * 128:(cg + 1) * 128]
            p_ref[pl.ds(p * 4 + cg, SLABS, stride=8), :] = piece


def middle(received, weights):
    return pl.pallas_call(
        middle_kernel,
        out_shape=pltpu.VMEM((SLABS * 8, 128), f32),
        scratch_shapes=[pltpu.VMEM((2 * KP, 256), f32), pltpu.VMEM((KP, 512), f32)],
        compiler_params=pltpu.CompilerParams(vmem_limit_bytes=VMEM_LIMIT),
        cost_estimate=pl.CostEstimate(flops=2 * 10**9, bytes_accessed=3 * 10**6, transcendentals=0),
        name="middle_modes",
    )(
        received,
        weights.transpose(0, 2, 1, 3),
        jnp.asarray(depth_forward_table()),
        jnp.asarray(expand_table()),
        jnp.asarray(collect_table()),
        jnp.asarray(depth_back_table()),
    )


def input_kernel(index_ref, r_ref, tz_ref, cut_ref, own_ref, first_ref, second_ref, third_ref, all_ref):
    u_real, u_imag = depth_modes(r_ref, 8, tz_ref)
    g_real, g_imag = depth_modes(r_ref, 0, tz_ref)
    real = jnp.concatenate([u_real, g_real], 0)
    imag = jnp.concatenate([u_imag, g_imag], 0)
    lanes = precise_dot(real, cut_ref[:256]) + precise_dot(imag, cut_ref[256:])
    for owner in range(4):
        for field in range(2):
            piece = lanes[field * KP:(field + 1) * KP, owner * 128:(owner + 1) * 128]
            all_ref[owner, :, field * 128:(field + 1) * 128] = piece
    me = index_ref[0]
    for k, ref in enumerate((own_ref, first_ref, second_ref, third_ref)):
        ref[...] = all_ref[me ^ k]


def input_modes(index, received):
    vmem = pl.BlockSpec(memory_space=pltpu.VMEM)
    return pl.pallas_call(
        input_kernel,
        out_shape=(jax.ShapeDtypeStruct((KP, 256), f32),) * 4,
        in_specs=[pl.BlockSpec(memory_space=pltpu.SMEM)] + [vmem] * 3,
        out_specs=(vmem,) * 4,
        scratch_shapes=[pltpu.VMEM((4, KP, 256), f32)],
        compiler_params=pltpu.CompilerParams(vmem_limit_bytes=VMEM_LIMIT),
        cost_estimate=pl.CostEstimate(flops=10**8, bytes_accessed=10**6, transcendentals=0),
        name="input_modes",
    )(index, received, jnp.asarray(depth_forward_table()), jnp.asarray(quarter_table()))


def weight_kernel(a_ref, b_ref, c_ref, d_ref, eu_ref, eg_ref, out_ref, u_ref, g_ref):
    mode = lane_iota(KP, 128) % 4
    for k, ref in enumerate((a_ref, b_ref, c_ref, d_ref)):
        for m in range(4):
            rows = pl.ds(k * 4 * KP + m, KP, stride=4)
            u_ref[rows, :] = jnp.where(mode == m, ref[:, :128], 0.0)
            g_ref[rows, :] = jnp.where(mode == m, ref[:, 128:], 0.0)
    u_all = precise_dot(u_ref[...], eu_ref[...])
    g_all = precise_dot(g_ref[...], eg_ref[...])
    real = jnp.zeros((4 * KP, 256), f32)
    imag = jnp.zeros((4 * KP, 256), f32)
    for k in range(4):
        cut = slice(k * 4 * KP, (k + 1) * 4 * KP)
        u_r, u_i = u_all[cut, :256], u_all[cut, 256:]
        g_r, g_i = g_all[cut, :256], g_all[cut, 256:]
        real = real + (u_r * g_r + u_i * g_i)
        imag = imag + (u_r * g_i - u_i * g_r)
    for kz in range(KZ):
        out_ref[0, kz] = real[kz * 4:(kz + 1) * 4]
        out_ref[1, kz] = imag[kz * 4:(kz + 1) * 4]


def weight_terms(pieces):
    return pl.pallas_call(
        weight_kernel,
        out_shape=pltpu.VMEM((2, KZ, 4, C * C), f32),
        scratch_shapes=[pltpu.VMEM((16 * KP, 128), f32), pltpu.VMEM((16 * KP, 128), f32)],
        compiler_params=pltpu.CompilerParams(vmem_limit_bytes=VMEM_LIMIT),
        cost_estimate=pl.CostEstimate(flops=2 * 10**9, bytes_accessed=2 * 10**6, transcendentals=0),
        name="weight_terms",
    )(*pieces, jnp.asarray(owned_table(0)), jnp.asarray(owned_table(1)))


def back_kernel(r_ref, ty_ref, tx_ref, terms_ref, out_hbm, terms_hbm, field_ref, q_ref, sems):
    copies = [pltpu.make_async_copy(terms_ref, terms_hbm, sems.at[32])]
    copies[0].start()
    highs, lows = [], []
    for half in range(2):
        rows = [r_ref[pl.ds(half * 8 + pg, KX, stride=16), :] for pg in range(8)]
        grid = jnp.concatenate(rows, 0)
        highs.append(grid.astype(bf16).astype(f32))
        lows.append(grid - highs[-1])
    parts = highs + lows
    place = lane_iota(256, 128) // 32

    def rows_x(c4):
        moved = [parts[t] if t == c4 else pltpu.roll(parts[t], (t - c4) % 4 * 32, 1) for t in range(4)]
        lanes = jnp.where(place == 0, moved[0], jnp.where(place == 1, moved[1], jnp.where(place == 2, moved[2], moved[3])))
        lanes = lanes.astype(bf16)
        high, low = split(dot(jnp.concatenate([lanes, lanes], 1), ty_ref[...]))
        for pg in range(8):
            for part in range(2):
                cut = (slice(pg * 32, (pg + 1) * 32), slice(part * 256, (part + 1) * 256))
                q_ref[c4, pg, part * 32:(part + 1) * 32, :] = high[cut]
                q_ref[c4, pg, 64 + part * 32:64 + (part + 1) * 32, :] = low[cut]

    rows_x(0)
    for c4 in range(4):
        for pg in range(8):
            if pg == 1 and c4 < 3:
                rows_x(c4 + 1)
            q = q_ref[c4, pg]
            field_ref[pg, c4] = dot(tx_ref[...], jnp.concatenate([q, q[:64]], 0)).astype(bf16)
            copies.append(pltpu.make_async_copy(field_ref.at[pg, c4], out_hbm.at[pg, c4], sems.at[c4 * 8 + pg]))
            copies[-1].start()
    for copy in copies:
        copy.wait()


def back(received, terms):
    vmem = pl.BlockSpec(memory_space=pltpu.VMEM)
    anywhere = pl.BlockSpec(memory_space=pl.ANY)
    field, terms = pl.pallas_call(
        back_kernel,
        out_shape=(
            jax.ShapeDtypeStruct((8, 4, NX, NY), bf16),
            jax.ShapeDtypeStruct((2, KZ, 4, C * C), f32),
        ),
        in_specs=[vmem] * 4,
        out_specs=(anywhere, anywhere),
        scratch_shapes=[
            pltpu.VMEM((8, 4, NX, NY), bf16),
            pltpu.VMEM((4, 8, 128, NY), bf16),
            pltpu.SemaphoreType.DMA((33,)),
        ],
        compiler_params=pltpu.CompilerParams(vmem_limit_bytes=VMEM_LIMIT),
        cost_estimate=pl.CostEstimate(flops=4 * 10**9, bytes_accessed=6 * 10**6, transcendentals=0),
        name="back_planes",
    )(received, jnp.asarray(y_back_table()), jnp.asarray(x_back_table()), terms)
    return field.reshape(1, 2, C, NX, NY), terms.transpose(0, 2, 1, 3)


def exchange(chunks, rows):
    moved = lax.all_to_all(chunks.reshape(SLABS, rows, 128), "slab", 0, 0, tiled=True)
    return moved.reshape(SLABS * rows, 128)


def body(field_in, cotangent, weights):
    index = lax.axis_index("group").astype(jnp.int32).reshape(1)
    received = exchange(forward(cotangent, field_in), 16)
    returned = exchange(middle(received, weights), 8)
    pieces = list(input_modes(index, received))
    for k in range(1, 4):
        pieces[k] = lax.ppermute(pieces[k], "group", [(i, i ^ k) for i in range(4)])
    return back(returned, weight_terms(pieces))


def solution(mesh):
    in_specs = (
        P("group", "slab", None, None, None),
        P("group", "slab", None, None, None),
        P(None, "slab", None, None),
    )
    out_specs = (P("group", "slab", None, None, None), P(None, ("slab", "group"), None, None))
    return jax.shard_map(body, mesh=mesh, in_specs=in_specs, out_specs=out_specs, check_vma=False)
```

```python
import math

import jax
import jax.numpy as jnp
import ml_dtypes
import numpy as np
from jax import lax
from jax.experimental import pallas as pl
from jax.experimental.pallas import tpu as pltpu
from jax.sharding import PartitionSpec as P

C = 16
KX = 32
KY = 32
KZ = 17
KP = 24
NX = 256
NY = 256
NZ = 128
SLABS = 64
HALF = KY // 2
SCALE = 1.0 / math.sqrt(NX * NY * NZ)
VMEM_LIMIT = 48 * 1024 * 1024

f32 = jnp.float32
bf16 = jnp.bfloat16


def kept_freqs(keep, length):
    index = np.arange(keep)
    return np.where(index < keep // 2, index, length - keep + index)


def phases(positions, freqs, length):
    turns = positions[:, None] * freqs[None, :] % length
    angle = turns.astype(np.float32) * np.float32(2.0 * math.pi / length)
    return angle.astype(np.float64)


def split_np(table):
    table = np.asarray(table, np.float32)
    high = table.astype(ml_dtypes.bfloat16)
    low = (table - high.astype(np.float32)).astype(ml_dtypes.bfloat16)
    return high, low


def x_forward_table():
    angle = phases(np.arange(NX), kept_freqs(KX, NX), NX)
    high, low = split_np(np.concatenate([np.cos(angle), np.sin(angle)], 1).T)
    return np.concatenate([high, low], 0)


def y_forward_table():
    angle = phases(np.arange(NY), kept_freqs(KY, NY), NY)
    real = np.cos(angle).astype(np.float32).astype(ml_dtypes.bfloat16)
    imag = (-np.sin(angle)).astype(np.float32).astype(ml_dtypes.bfloat16)
    lanes = []
    for half in range(2):
        for part in (real, imag):
            lanes.extend([part[:, half * HALF:(half + 1) * HALF]] * 4)
    return np.concatenate(lanes, 1)


def depth_positions():
    s = np.arange(SLABS)
    return np.concatenate([2 * s, 2 * s + 1])


def depth_forward_table():
    angle = phases(depth_positions(), np.arange(KZ), NZ)
    table = np.zeros((2 * KP, NZ), np.float32)
    table[:KZ] = np.cos(angle).T
    table[KP:KP + KZ] = np.sin(angle).T
    high, low = split_np(table)
    return np.concatenate([high, high, low], 1)


def depth_back_table():
    angle = phases(depth_positions(), np.arange(KZ), NZ)
    table = np.zeros((NZ, 2 * KP), np.float32)
    table[:, :KZ] = np.cos(angle)
    table[:, KP:KP + KZ] = np.sin(angle)
    high, low = split_np(table)
    return np.concatenate([high, high, low], 1)


def channel_mode_lanes():
    lane = np.arange(256)
    return lane // 16, lane % 16


def expand_table():
    c, _ = channel_mode_lanes()
    col = np.arange(256)
    return (c[:, None] == (col % 16)[None]).astype(ml_dtypes.bfloat16)


def collect_table():
    row, col = np.arange(512), np.arange(512)
    channel = col // 128 * 4 + col // 32 % 4
    hit = (row // 256)[:, None] == (col // 16 % 2)[None]
    return (hit & ((row // 16 % 16)[:, None] == channel[None])).astype(ml_dtypes.bfloat16)


def quarter_table():
    c, ky = channel_mode_lanes()
    table = np.zeros((2, 256, 512), np.float32)
    for part in range(2):
        table[part, np.arange(256), ky // 4 * 128 + part * 64 + c * 4 + ky % 4] = 1.0
    return table.reshape(512, 512).astype(ml_dtypes.bfloat16)


def owned_table(which):
    row, col = np.arange(128), np.arange(512)
    target = col // 16 % 16 if which == 0 else col % 16
    hit = (row // 64)[:, None] == (col // 256)[None]
    return (hit & ((row // 4 % 16)[:, None] == target[None])).astype(ml_dtypes.bfloat16)


def y_back_table():
    angle = phases(kept_freqs(KY, NY), np.arange(NY), NY)
    cos, sin = np.cos(angle), np.sin(angle)
    rows = []
    for half in range(2):
        cut = slice(half * HALF, (half + 1) * HALF)
        rows.append(np.concatenate([cos[cut], sin[cut]], 1))
        rows.append(np.concatenate([-sin[cut], cos[cut]], 1))
    high, low = split_np(np.concatenate(rows, 0))
    return np.concatenate([high, high, low, np.zeros_like(low)], 0)


def x_back_table():
    angle = phases(np.arange(NX), kept_freqs(KX, NX), NX)
    table = np.concatenate([np.cos(angle), -np.sin(angle)], 1) * SCALE
    high, low = split_np(table)
    return np.concatenate([high, high, low], 1)


def dot(left, right):
    return jnp.dot(left, right, preferred_element_type=f32)


def split(value):
    high = value.astype(bf16)
    low = (value - high.astype(f32)).astype(bf16)
    return high, low


def lane_iota(rows, lanes):
    return lax.broadcasted_iota(jnp.int32, (rows, lanes), 1)


def swap_parts(value):
    tiles = [pltpu.roll(value[:, t * 128:(t + 1) * 128], 64, 1) for t in range(value.shape[1] // 128)]
    return jnp.concatenate(tiles, 1)


STEPS = 16
WAITS = (2, 3, 4, 7)


def forward_kernel(cot_hbm, fld_hbm, tx_hbm, ty_hbm, out_ref, field_ref, tx_ref, ty_ref, rows_ref, sems):
    tables = [
        pltpu.make_async_copy(ty_hbm, ty_ref, sems.at[STEPS]),
        pltpu.make_async_copy(tx_hbm, tx_ref, sems.at[STEPS + 1]),
    ]
    blocks = []
    for i in range(STEPS):
        source = cot_hbm if i < 8 else fld_hbm
        blocks.append(pltpu.make_async_copy(source.at[pl.ds(i % 8 * 4, 4)], field_ref.at[pl.ds(i * 4, 4)], sems.at[i]))
    for copy in tables + blocks:
        copy.start()
    for copy in tables:
        copy.wait()
    slot = lane_iota(NX, 256) // 16 % 4
    sign = jnp.where(lane_iota(KX, 256) % 128 < 64, 1.0, -1.0)

    def rows_y(i):
        parts = [dot(field_ref[i * 4 + c4], ty_ref[...]) for c4 in range(4)]
        rows = jnp.where(slot == 0, parts[0], jnp.where(slot == 1, parts[1], jnp.where(slot == 2, parts[2], parts[3])))
        high, low = split(rows)
        rows_ref[0, :, i * 256:(i + 1) * 256] = high
        rows_ref[1, :, i * 256:(i + 1) * 256] = low

    def spectra(start, count):
        lanes = slice(start * 256, (start + count) * 256)
        mixed = dot(tx_ref[...], rows_ref[0, :, lanes])
        mixed = mixed[:64] + mixed[64:] + dot(tx_ref[:64], rows_ref[1, :, lanes])
        for j in range(count):
            both = mixed[:, j * 256:(j + 1) * 256]
            result = both[:KX] + sign * swap_parts(both[KX:])
            for half in range(2):
                row = half * 16 + start + j
                out_ref[pl.ds(row, KX, stride=32), :] = result[:, half * 128:(half + 1) * 128]

    first, ready = 0, (0, 0)
    for count in WAITS:
        for i in range(first, first + count):
            blocks[i].wait()
        for i in range(first, first + count):
            rows_y(i)
        if ready[1]:
            spectra(*ready)
        ready = (first, count)
        first += count
    spectra(*ready)


def forward(cotangent, field_in):
    anywhere = pl.BlockSpec(memory_space=pl.ANY)
    return pl.pallas_call(
        forward_kernel,
        out_shape=pltpu.VMEM((SLABS * 16, 128), f32),
        in_specs=[anywhere] * 4,
        scratch_shapes=[
            pltpu.VMEM((STEPS * 4, NX, NY), bf16),
            pltpu.VMEM((128, NX), bf16),
            pltpu.VMEM((NY, 256), bf16),
            pltpu.VMEM((2, NX, STEPS * 256), bf16),
            pltpu.SemaphoreType.DMA((STEPS + 2,)),
        ],
        compiler_params=pltpu.CompilerParams(vmem_limit_bytes=60 * 1024 * 1024),
        cost_estimate=pl.CostEstimate(flops=4 * 10**9, bytes_accessed=9 * 10**6, transcendentals=0),
        name="forward_planes",
    )(
        cotangent.reshape(2 * C, NX, NY),
        field_in.reshape(2 * C, NX, NY),
        jnp.asarray(x_forward_table()),
        jnp.asarray(y_forward_table()),
    )


def roll_half(value):
    return pltpu.roll(value, 64, 1)


def depth_modes(r_ref, first, tz_ref):
    tiles = []
    for cg in range(4):
        rows = [r_ref[pl.ds(first + p * 4 + cg, SLABS, stride=16), :] for p in range(2)]
        tiles.append(jnp.concatenate(rows, 0))
    high, low = split(jnp.concatenate(tiles, 1))
    both = dot(tz_ref[...], jnp.concatenate([high, low, high], 0)) * SCALE
    left = lane_iota(KP, 128) < 64
    real, imag = [], []
    for pair in range(2):
        cuts = [slice((2 * pair + j) * 128, (2 * pair + j + 1) * 128) for j in range(2)]
        c0, c1 = both[:KP, cuts[0]], both[:KP, cuts[1]]
        s0, s1 = both[KP:, cuts[0]], both[KP:, cuts[1]]
        real.append(jnp.where(left, c0 + roll_half(s0), roll_half(c1) + s1))
        imag.append(jnp.where(left, roll_half(c0) - s0, c1 - roll_half(s1)))
    return jnp.concatenate(real, 1), jnp.concatenate(imag, 1)


def precise_dot(value, table):
    high, low = split(value)
    both = dot(jnp.concatenate([high, low], 0), table)
    return both[:value.shape[0]] + both[value.shape[0]:]


def middle_kernel(r_ref, w_ref, tz_ref, e_ref, c_ref, tb_ref, p_ref, g_ref, sum_ref):
    g_real, g_imag = depth_modes(r_ref, 0, tz_ref)
    g_ref[:KP] = g_real
    g_ref[KP:] = g_imag
    own = lane_iota(HALF, 256) % 16 == lax.broadcasted_iota(jnp.int32, (HALF, 256), 0)
    rows = []
    for part in range(2):
        for kz in range(KZ):
            line = g_ref[part * KP + kz:part * KP + kz + 1, :]
            rows.append(jnp.where(own, jnp.broadcast_to(line, (HALF, 256)), 0.0))
    wide = precise_dot(jnp.concatenate(rows, 0), e_ref[...])
    products = []
    for kz in range(KZ):
        g_r = wide[kz * HALF:(kz + 1) * HALF]
        g_i = wide[(KZ + kz) * HALF:(KZ + kz + 1) * HALF]
        w_r, w_i = w_ref[0, kz].astype(f32), w_ref[1, kz].astype(f32)
        products.append(jnp.concatenate([g_r * w_r + g_i * w_i, g_i * w_r - g_r * w_i], 1))
    sums = precise_dot(jnp.concatenate(products, 0), c_ref[...])
    own = jnp.concatenate([own, own], 1)
    sum_ref[...] = jnp.zeros_like(sum_ref)
    for kz in range(KZ):
        kept = jnp.where(own, sums[kz * HALF:(kz + 1) * HALF], 0.0)
        sum_ref[kz:kz + 1, :] = jnp.sum(kept, axis=0, keepdims=True)
    direct = sum_ref[...]
    real_lane = lane_iota(KP, 128) % 32 < 16
    turned = []
    for cg in range(4):
        tile = direct[:, cg * 128:(cg + 1) * 128]
        turned.append(jnp.where(real_lane, -pltpu.roll(tile, 112, 1), pltpu.roll(tile, 16, 1)))
    stacked = jnp.concatenate([direct, jnp.concatenate(turned, 1)], 0)
    high, low = split(stacked)
    planes = dot(tb_ref[...], jnp.concatenate([high, low, high], 0))
    for p in range(2):
        for cg in range(4):
            piece = planes[p * SLABS:(p + 1) * SLABS, cg * 128:(cg + 1) * 128]
            p_ref[pl.ds(p * 4 + cg, SLABS, stride=8), :] = piece


def middle(received, weights):
    return pl.pallas_call(
        middle_kernel,
        out_shape=pltpu.VMEM((SLABS * 8, 128), f32),
        scratch_shapes=[pltpu.VMEM((2 * KP, 256), f32), pltpu.VMEM((KP, 512), f32)],
        compiler_params=pltpu.CompilerParams(vmem_limit_bytes=VMEM_LIMIT),
        cost_estimate=pl.CostEstimate(flops=2 * 10**9, bytes_accessed=3 * 10**6, transcendentals=0),
        name="middle_modes",
    )(
        received,
        weights.transpose(0, 2, 1, 3),
        jnp.asarray(depth_forward_table()),
        jnp.asarray(expand_table()),
        jnp.asarray(collect_table()),
        jnp.asarray(depth_back_table()),
    )


def input_kernel(index_ref, r_ref, tz_ref, cut_ref, own_ref, first_ref, second_ref, third_ref, all_ref):
    u_real, u_imag = depth_modes(r_ref, 8, tz_ref)
    g_real, g_imag = depth_modes(r_ref, 0, tz_ref)
    real = jnp.concatenate([u_real, g_real], 0)
    imag = jnp.concatenate([u_imag, g_imag], 0)
    lanes = precise_dot(real, cut_ref[:256]) + precise_dot(imag, cut_ref[256:])
    for owner in range(4):
        for field in range(2):
            piece = lanes[field * KP:(field + 1) * KP, owner * 128:(owner + 1) * 128]
            all_ref[owner, :, field * 128:(field + 1) * 128] = piece
    me = index_ref[0]
    for k, ref in enumerate((own_ref, first_ref, second_ref, third_ref)):
        ref[...] = all_ref[me ^ k]


def input_modes(index, received):
    vmem = pl.BlockSpec(memory_space=pltpu.VMEM)
    return pl.pallas_call(
        input_kernel,
        out_shape=(jax.ShapeDtypeStruct((KP, 256), f32),) * 4,
        in_specs=[pl.BlockSpec(memory_space=pltpu.SMEM)] + [vmem] * 3,
        out_specs=(vmem,) * 4,
        scratch_shapes=[pltpu.VMEM((4, KP, 256), f32)],
        compiler_params=pltpu.CompilerParams(vmem_limit_bytes=VMEM_LIMIT),
        cost_estimate=pl.CostEstimate(flops=10**8, bytes_accessed=10**6, transcendentals=0),
        name="input_modes",
    )(index, received, jnp.asarray(depth_forward_table()), jnp.asarray(quarter_table()))


def weight_kernel(a_ref, b_ref, c_ref, d_ref, eu_ref, eg_ref, out_ref, u_ref, g_ref):
    mode = lane_iota(KP, 128) % 4
    for k, ref in enumerate((a_ref, b_ref, c_ref, d_ref)):
        for m in range(4):
            rows = pl.ds(k * 4 * KP + m, KP, stride=4)
            u_ref[rows, :] = jnp.where(mode == m, ref[:, :128], 0.0)
            g_ref[rows, :] = jnp.where(mode == m, ref[:, 128:], 0.0)
    u_all = precise_dot(u_ref[...], eu_ref[...])
    g_all = precise_dot(g_ref[...], eg_ref[...])
    real = jnp.zeros((4 * KP, 256), f32)
    imag = jnp.zeros((4 * KP, 256), f32)
    for k in range(4):
        cut = slice(k * 4 * KP, (k + 1) * 4 * KP)
        u_r, u_i = u_all[cut, :256], u_all[cut, 256:]
        g_r, g_i = g_all[cut, :256], g_all[cut, 256:]
        real = real + (u_r * g_r + u_i * g_i)
        imag = imag + (u_r * g_i - u_i * g_r)
    for kz in range(KZ):
        out_ref[0, kz] = real[kz * 4:(kz + 1) * 4]
        out_ref[1, kz] = imag[kz * 4:(kz + 1) * 4]


def weight_terms(pieces):
    return pl.pallas_call(
        weight_kernel,
        out_shape=pltpu.VMEM((2, KZ, 4, C * C), f32),
        scratch_shapes=[pltpu.VMEM((16 * KP, 128), f32), pltpu.VMEM((16 * KP, 128), f32)],
        compiler_params=pltpu.CompilerParams(vmem_limit_bytes=VMEM_LIMIT),
        cost_estimate=pl.CostEstimate(flops=2 * 10**9, bytes_accessed=2 * 10**6, transcendentals=0),
        name="weight_terms",
    )(*pieces, jnp.asarray(owned_table(0)), jnp.asarray(owned_table(1)))


def back_kernel(r_ref, ty_ref, tx_ref, terms_ref, out_hbm, terms_hbm, field_ref, q_ref, sems):
    copies = [pltpu.make_async_copy(terms_ref, terms_hbm, sems.at[32])]
    copies[0].start()
    highs, lows = [], []
    for half in range(2):
        rows = [r_ref[pl.ds(half * 8 + pg, KX, stride=16), :] for pg in range(8)]
        grid = jnp.concatenate(rows, 0)
        highs.append(grid.astype(bf16).astype(f32))
        lows.append(grid - highs[-1])
    parts = highs + lows
    place = lane_iota(256, 128) // 32

    def rows_x(c4):
        moved = [parts[t] if t == c4 else pltpu.roll(parts[t], (t - c4) % 4 * 32, 1) for t in range(4)]
        lanes = jnp.where(place == 0, moved[0], jnp.where(place == 1, moved[1], jnp.where(place == 2, moved[2], moved[3])))
        lanes = lanes.astype(bf16)
        high, low = split(dot(jnp.concatenate([lanes, lanes], 1), ty_ref[...]))
        for pg in range(8):
            for part in range(2):
                cut = (slice(pg * 32, (pg + 1) * 32), slice(part * 256, (part + 1) * 256))
                q_ref[c4, pg, part * 32:(part + 1) * 32, :] = high[cut]
                q_ref[c4, pg, 64 + part * 32:64 + (part + 1) * 32, :] = low[cut]

    rows_x(0)
    for c4 in range(4):
        for pg in range(8):
            if pg == 1 and c4 < 3:
                rows_x(c4 + 1)
            q = q_ref[c4, pg]
            field_ref[pg, c4] = dot(tx_ref[...], jnp.concatenate([q, q[:64]], 0)).astype(bf16)
            copies.append(pltpu.make_async_copy(field_ref.at[pg, c4], out_hbm.at[pg, c4], sems.at[c4 * 8 + pg]))
            copies[-1].start()
    for copy in copies:
        copy.wait()


def back(received, terms):
    vmem = pl.BlockSpec(memory_space=pltpu.VMEM)
    anywhere = pl.BlockSpec(memory_space=pl.ANY)
    field, terms = pl.pallas_call(
        back_kernel,
        out_shape=(
            jax.ShapeDtypeStruct((8, 4, NX, NY), bf16),
            jax.ShapeDtypeStruct((2, KZ, 4, C * C), f32),
        ),
        in_specs=[vmem] * 4,
        out_specs=(anywhere, anywhere),
        scratch_shapes=[
            pltpu.VMEM((8, 4, NX, NY), bf16),
            pltpu.VMEM((4, 8, 128, NY), bf16),
            pltpu.SemaphoreType.DMA((33,)),
        ],
        compiler_params=pltpu.CompilerParams(vmem_limit_bytes=VMEM_LIMIT),
        cost_estimate=pl.CostEstimate(flops=4 * 10**9, bytes_accessed=6 * 10**6, transcendentals=0),
        name="back_planes",
    )(received, jnp.asarray(y_back_table()), jnp.asarray(x_back_table()), terms)
    return field.reshape(1, 2, C, NX, NY), terms.transpose(0, 2, 1, 3)


def exchange(chunks, rows):
    moved = lax.all_to_all(chunks.reshape(SLABS, rows, 128), "slab", 0, 0, tiled=True)
    return moved.reshape(SLABS * rows, 128)


def body(field_in, cotangent, weights):
    index = lax.axis_index("group").astype(jnp.int32).reshape(1)
    received = exchange(forward(cotangent, field_in), 16)
    returned = exchange(middle(received, weights), 8)
    pieces = list(input_modes(index, received))
    for k in range(1, 4):
        pieces[k] = lax.ppermute(pieces[k], "group", [(i, i ^ k) for i in range(4)])
    return back(returned, weight_terms(pieces))


def solution(mesh):
    in_specs = (
        P("group", "slab", None, None, None),
        P("group", "slab", None, None, None),
        P(None, "slab", None, None),
    )
    out_specs = (P("group", "slab", None, None, None), P(None, ("slab", "group"), None, None))
    return jax.shard_map(body, mesh=mesh, in_specs=in_specs, out_specs=out_specs, check_vma=False)
```

```python
import math

import jax
import jax.numpy as jnp
import ml_dtypes
import numpy as np
from jax import lax
from jax.experimental import pallas as pl
from jax.experimental.pallas import tpu as pltpu
from jax.sharding import PartitionSpec as P

C = 16
KX = 32
KY = 32
KZ = 17
KP = 24
NX = 256
NY = 256
NZ = 128
SLABS = 64
HALF = KY // 2
SCALE = 1.0 / math.sqrt(NX * NY * NZ)
VMEM_LIMIT = 48 * 1024 * 1024

f32 = jnp.float32
bf16 = jnp.bfloat16


def kept_freqs(keep, length):
    index = np.arange(keep)
    return np.where(index < keep // 2, index, length - keep + index)


def phases(positions, freqs, length):
    turns = positions[:, None] * freqs[None, :] % length
    angle = turns.astype(np.float32) * np.float32(2.0 * math.pi / length)
    return angle.astype(np.float64)


def split_np(table):
    table = np.asarray(table, np.float32)
    high = table.astype(ml_dtypes.bfloat16)
    low = (table - high.astype(np.float32)).astype(ml_dtypes.bfloat16)
    return high, low


def x_forward_table():
    angle = phases(np.arange(NX), kept_freqs(KX, NX), NX)
    high, low = split_np(np.concatenate([np.cos(angle), np.sin(angle)], 1).T)
    return np.concatenate([high, low], 0)


def y_forward_table():
    angle = phases(np.arange(NY), kept_freqs(KY, NY), NY)
    real = np.cos(angle).astype(np.float32).astype(ml_dtypes.bfloat16)
    imag = (-np.sin(angle)).astype(np.float32).astype(ml_dtypes.bfloat16)
    lanes = []
    for half in range(2):
        for part in (real, imag):
            lanes.extend([part[:, half * HALF:(half + 1) * HALF]] * 4)
    return np.concatenate(lanes, 1)


def depth_positions():
    s = np.arange(SLABS)
    return np.concatenate([2 * s, 2 * s + 1])


def depth_forward_table():
    angle = phases(depth_positions(), np.arange(KZ), NZ)
    table = np.zeros((2 * KP, NZ), np.float32)
    table[:KZ] = np.cos(angle).T
    table[KP:KP + KZ] = np.sin(angle).T
    high, low = split_np(table)
    return np.concatenate([high, high, low], 1)


def depth_back_table():
    angle = phases(depth_positions(), np.arange(KZ), NZ)
    table = np.zeros((NZ, 2 * KP), np.float32)
    table[:, :KZ] = np.cos(angle)
    table[:, KP:KP + KZ] = np.sin(angle)
    high, low = split_np(table)
    return np.concatenate([high, high, low], 1)


def channel_mode_lanes():
    lane = np.arange(256)
    return lane // 16, lane % 16


def expand_table():
    c, _ = channel_mode_lanes()
    col = np.arange(256)
    return (c[:, None] == (col % 16)[None]).astype(ml_dtypes.bfloat16)


def collect_table():
    row, col = np.arange(256), np.arange(256)
    hit = (row // 128)[:, None] == (col // 128)[None]
    hit = hit & ((row // 64 % 2)[:, None] == (col // 16 % 2)[None])
    return (hit & ((row // 16 % 4)[:, None] == (col // 32 % 4)[None])).astype(ml_dtypes.bfloat16)


def quarter_table():
    c, ky = channel_mode_lanes()
    table = np.zeros((2, 256, 512), np.float32)
    for part in range(2):
        table[part, np.arange(256), ky // 4 * 128 + part * 64 + c * 4 + ky % 4] = 1.0
    return table.reshape(512, 512).astype(ml_dtypes.bfloat16)


def owned_table(which):
    row, col = np.arange(128), np.arange(512)
    target = col // 16 % 16 if which == 0 else col % 16
    hit = (row // 64)[:, None] == (col // 256)[None]
    return (hit & ((row // 4 % 16)[:, None] == target[None])).astype(ml_dtypes.bfloat16)


def y_back_table():
    angle = phases(kept_freqs(KY, NY), np.arange(NY), NY)
    cos, sin = np.cos(angle), np.sin(angle)
    rows = []
    for half in range(2):
        cut = slice(half * HALF, (half + 1) * HALF)
        rows.append(np.concatenate([cos[cut], sin[cut]], 1))
        rows.append(np.concatenate([-sin[cut], cos[cut]], 1))
    high, low = split_np(np.concatenate(rows, 0))
    return np.concatenate([high, high, low, np.zeros_like(low)], 0)


def x_back_table():
    angle = phases(np.arange(NX), kept_freqs(KX, NX), NX)
    table = np.concatenate([np.cos(angle), -np.sin(angle)], 1) * SCALE
    high, low = split_np(table)
    return np.concatenate([high, high, low], 1)


def dot(left, right):
    return jnp.dot(left, right, preferred_element_type=f32)


def split(value):
    high = value.astype(bf16)
    low = (value - high.astype(f32)).astype(bf16)
    return high, low


def lane_iota(rows, lanes):
    return lax.broadcasted_iota(jnp.int32, (rows, lanes), 1)


def swap_parts(value):
    tiles = [pltpu.roll(value[:, t * 128:(t + 1) * 128], 64, 1) for t in range(value.shape[1] // 128)]
    return jnp.concatenate(tiles, 1)


STEPS = 16
WAITS = (2, 3, 4, 7)


def forward_kernel(cot_hbm, fld_hbm, tx_hbm, ty_hbm, out_ref, field_ref, tx_ref, ty_ref, rows_ref, sems):
    tables = [
        pltpu.make_async_copy(ty_hbm, ty_ref, sems.at[STEPS]),
        pltpu.make_async_copy(tx_hbm, tx_ref, sems.at[STEPS + 1]),
    ]
    blocks = []
    for i in range(STEPS):
        source = cot_hbm if i < 8 else fld_hbm
        blocks.append(pltpu.make_async_copy(source.at[pl.ds(i % 8 * 4, 4)], field_ref.at[pl.ds(i * 4, 4)], sems.at[i]))
    for copy in tables + blocks:
        copy.start()
    for copy in tables:
        copy.wait()
    slot = lane_iota(NX, 256) // 16 % 4
    sign = jnp.where(lane_iota(KX, 256) % 128 < 64, 1.0, -1.0)

    def rows_y(i):
        parts = [dot(field_ref[i * 4 + c4], ty_ref[...]) for c4 in range(4)]
        rows = jnp.where(slot == 0, parts[0], jnp.where(slot == 1, parts[1], jnp.where(slot == 2, parts[2], parts[3])))
        high, low = split(rows)
        rows_ref[0, :, i * 256:(i + 1) * 256] = high
        rows_ref[1, :, i * 256:(i + 1) * 256] = low

    def spectra(start, count):
        lanes = slice(start * 256, (start + count) * 256)
        mixed = dot(tx_ref[...], rows_ref[0, :, lanes])
        mixed = mixed[:64] + mixed[64:] + dot(tx_ref[:64], rows_ref[1, :, lanes])
        for j in range(count):
            both = mixed[:, j * 256:(j + 1) * 256]
            result = both[:KX] + sign * swap_parts(both[KX:])
            for half in range(2):
                row = half * 16 + start + j
                out_ref[pl.ds(row, KX, stride=32), :] = result[:, half * 128:(half + 1) * 128]

    first, ready = 0, (0, 0)
    for count in WAITS:
        for i in range(first, first + count):
            blocks[i].wait()
        for i in range(first, first + count):
            rows_y(i)
        if ready[1]:
            spectra(*ready)
        ready = (first, count)
        first += count
    spectra(*ready)


def forward(cotangent, field_in):
    anywhere = pl.BlockSpec(memory_space=pl.ANY)
    return pl.pallas_call(
        forward_kernel,
        out_shape=pltpu.VMEM((SLABS * 16, 128), f32),
        in_specs=[anywhere] * 4,
        scratch_shapes=[
            pltpu.VMEM((STEPS * 4, NX, NY), bf16),
            pltpu.VMEM((128, NX), bf16),
            pltpu.VMEM((NY, 256), bf16),
            pltpu.VMEM((2, NX, STEPS * 256), bf16),
            pltpu.SemaphoreType.DMA((STEPS + 2,)),
        ],
        compiler_params=pltpu.CompilerParams(vmem_limit_bytes=60 * 1024 * 1024),
        cost_estimate=pl.CostEstimate(flops=4 * 10**9, bytes_accessed=9 * 10**6, transcendentals=0),
        name="forward_planes",
    )(
        cotangent.reshape(2 * C, NX, NY),
        field_in.reshape(2 * C, NX, NY),
        jnp.asarray(x_forward_table()),
        jnp.asarray(y_forward_table()),
    )


def roll_half(value):
    return pltpu.roll(value, 64, 1)


def depth_modes(r_ref, first, tz_ref):
    tiles = []
    for cg in range(4):
        rows = [r_ref[pl.ds(first + p * 4 + cg, SLABS, stride=16), :] for p in range(2)]
        tiles.append(jnp.concatenate(rows, 0))
    high, low = split(jnp.concatenate(tiles, 1))
    both = dot(tz_ref[...], jnp.concatenate([high, low, high], 0)) * SCALE
    left = lane_iota(KP, 128) < 64
    real, imag = [], []
    for pair in range(2):
        cuts = [slice((2 * pair + j) * 128, (2 * pair + j + 1) * 128) for j in range(2)]
        c0, c1 = both[:KP, cuts[0]], both[:KP, cuts[1]]
        s0, s1 = both[KP:, cuts[0]], both[KP:, cuts[1]]
        real.append(jnp.where(left, c0 + roll_half(s0), roll_half(c1) + s1))
        imag.append(jnp.where(left, roll_half(c0) - s0, c1 - roll_half(s1)))
    return jnp.concatenate(real, 1), jnp.concatenate(imag, 1)


def precise_dot(value, table):
    high, low = split(value)
    both = dot(jnp.concatenate([high, low], 0), table)
    return both[:value.shape[0]] + both[value.shape[0]:]


def middle_kernel(r_ref, w_ref, tz_ref, e_ref, c_ref, tb_ref, p_ref, g_ref, sum_ref):
    g_real, g_imag = depth_modes(r_ref, 0, tz_ref)
    g_ref[:KP] = g_real
    g_ref[KP:] = g_imag
    own = lane_iota(HALF, 256) % 16 == lax.broadcasted_iota(jnp.int32, (HALF, 256), 0)
    rows = []
    for part in range(2):
        for kz in range(KZ):
            line = g_ref[part * KP + kz:part * KP + kz + 1, :]
            rows.append(jnp.where(own, jnp.broadcast_to(line, (HALF, 256)), 0.0))
    wide = precise_dot(jnp.concatenate(rows, 0), e_ref[...])
    products = []
    for kz in range(KZ):
        g_r = wide[kz * HALF:(kz + 1) * HALF]
        g_i = wide[(KZ + kz) * HALF:(KZ + kz + 1) * HALF]
        w_r, w_i = w_ref[0, kz].astype(f32), w_ref[1, kz].astype(f32)
        products.append((g_r * w_r + g_i * w_i, g_i * w_r - g_r * w_i))
    left_half = lane_iota(HALF, 128) < 64
    halves = []
    for pair in range(2):
        cut = slice(pair * 128, (pair + 1) * 128)
        for real, imag in products:
            first = jnp.where(left_half, real[:, cut], roll_half(imag[:, cut]))
            second = jnp.where(left_half, roll_half(real[:, cut]), imag[:, cut])
            halves.append(jnp.concatenate([first, second], 1))
    sums = precise_dot(jnp.concatenate(halves, 0), c_ref[...])
    sums = jnp.concatenate([sums[:KZ * HALF], sums[KZ * HALF:]], 1)
    own = jnp.concatenate([own, own], 1)
    sum_ref[...] = jnp.zeros_like(sum_ref)
    for kz in range(KZ):
        kept = jnp.where(own, sums[kz * HALF:(kz + 1) * HALF], 0.0)
        sum_ref[kz:kz + 1, :] = jnp.sum(kept, axis=0, keepdims=True)
    direct = sum_ref[...]
    real_lane = lane_iota(KP, 128) % 32 < 16
    turned = []
    for cg in range(4):
        tile = direct[:, cg * 128:(cg + 1) * 128]
        turned.append(jnp.where(real_lane, -pltpu.roll(tile, 112, 1), pltpu.roll(tile, 16, 1)))
    stacked = jnp.concatenate([direct, jnp.concatenate(turned, 1)], 0)
    high, low = split(stacked)
    planes = dot(tb_ref[...], jnp.concatenate([high, low, high], 0))
    for p in range(2):
        for cg in range(4):
            piece = planes[p * SLABS:(p + 1) * SLABS, cg * 128:(cg + 1) * 128]
            p_ref[pl.ds(p * 4 + cg, SLABS, stride=8), :] = piece


def middle(received, weights):
    return pl.pallas_call(
        middle_kernel,
        out_shape=pltpu.VMEM((SLABS * 8, 128), f32),
        scratch_shapes=[pltpu.VMEM((2 * KP, 256), f32), pltpu.VMEM((KP, 512), f32)],
        compiler_params=pltpu.CompilerParams(vmem_limit_bytes=VMEM_LIMIT),
        cost_estimate=pl.CostEstimate(flops=2 * 10**9, bytes_accessed=3 * 10**6, transcendentals=0),
        name="middle_modes",
    )(
        received,
        weights.transpose(0, 2, 1, 3),
        jnp.asarray(depth_forward_table()),
        jnp.asarray(expand_table()),
        jnp.asarray(collect_table()),
        jnp.asarray(depth_back_table()),
    )


def input_kernel(index_ref, r_ref, tz_ref, cut_ref, own_ref, first_ref, second_ref, third_ref, all_ref):
    u_real, u_imag = depth_modes(r_ref, 8, tz_ref)
    g_real, g_imag = depth_modes(r_ref, 0, tz_ref)
    real = jnp.concatenate([u_real, g_real], 0)
    imag = jnp.concatenate([u_imag, g_imag], 0)
    lanes = precise_dot(real, cut_ref[:256]) + precise_dot(imag, cut_ref[256:])
    for owner in range(4):
        for field in range(2):
            piece = lanes[field * KP:(field + 1) * KP, owner * 128:(owner + 1) * 128]
            all_ref[owner, :, field * 128:(field + 1) * 128] = piece
    me = index_ref[0]
    for k, ref in enumerate((own_ref, first_ref, second_ref, third_ref)):
        ref[...] = all_ref[me ^ k]


def input_modes(index, received):
    vmem = pl.BlockSpec(memory_space=pltpu.VMEM)
    return pl.pallas_call(
        input_kernel,
        out_shape=(jax.ShapeDtypeStruct((KP, 256), f32),) * 4,
        in_specs=[pl.BlockSpec(memory_space=pltpu.SMEM)] + [vmem] * 3,
        out_specs=(vmem,) * 4,
        scratch_shapes=[pltpu.VMEM((4, KP, 256), f32)],
        compiler_params=pltpu.CompilerParams(vmem_limit_bytes=VMEM_LIMIT),
        cost_estimate=pl.CostEstimate(flops=10**8, bytes_accessed=10**6, transcendentals=0),
        name="input_modes",
    )(index, received, jnp.asarray(depth_forward_table()), jnp.asarray(quarter_table()))


def weight_kernel(a_ref, b_ref, c_ref, d_ref, eu_ref, eg_ref, out_ref, u_ref, g_ref):
    mode = lane_iota(KP, 128) % 4
    for k, ref in enumerate((a_ref, b_ref, c_ref, d_ref)):
        for m in range(4):
            rows = pl.ds(k * 4 * KP + m, KP, stride=4)
            u_ref[rows, :] = jnp.where(mode == m, ref[:, :128], 0.0)
            g_ref[rows, :] = jnp.where(mode == m, ref[:, 128:], 0.0)
    u_all = precise_dot(u_ref[...], eu_ref[...])
    g_all = precise_dot(g_ref[...], eg_ref[...])
    real = jnp.zeros((4 * KP, 256), f32)
    imag = jnp.zeros((4 * KP, 256), f32)
    for k in range(4):
        cut = slice(k * 4 * KP, (k + 1) * 4 * KP)
        u_r, u_i = u_all[cut, :256], u_all[cut, 256:]
        g_r, g_i = g_all[cut, :256], g_all[cut, 256:]
        real = real + (u_r * g_r + u_i * g_i)
        imag = imag + (u_r * g_i - u_i * g_r)
    for kz in range(KZ):
        out_ref[0, kz] = real[kz * 4:(kz + 1) * 4]
        out_ref[1, kz] = imag[kz * 4:(kz + 1) * 4]


def weight_terms(pieces):
    return pl.pallas_call(
        weight_kernel,
        out_shape=pltpu.VMEM((2, KZ, 4, C * C), f32),
        scratch_shapes=[pltpu.VMEM((16 * KP, 128), f32), pltpu.VMEM((16 * KP, 128), f32)],
        compiler_params=pltpu.CompilerParams(vmem_limit_bytes=VMEM_LIMIT),
        cost_estimate=pl.CostEstimate(flops=2 * 10**9, bytes_accessed=2 * 10**6, transcendentals=0),
        name="weight_terms",
    )(*pieces, jnp.asarray(owned_table(0)), jnp.asarray(owned_table(1)))


def back_kernel(r_ref, ty_ref, tx_ref, terms_ref, out_hbm, terms_hbm, field_ref, q_ref, sems):
    copies = [pltpu.make_async_copy(terms_ref, terms_hbm, sems.at[32])]
    copies[0].start()
    highs, lows = [], []
    for half in range(2):
        rows = [r_ref[pl.ds(half * 8 + pg, KX, stride=16), :] for pg in range(8)]
        grid = jnp.concatenate(rows, 0)
        highs.append(grid.astype(bf16).astype(f32))
        lows.append(grid - highs[-1])
    parts = highs + lows
    place = lane_iota(256, 128) // 32

    def rows_x(c4):
        moved = [parts[t] if t == c4 else pltpu.roll(parts[t], (t - c4) % 4 * 32, 1) for t in range(4)]
        lanes = jnp.where(place == 0, moved[0], jnp.where(place == 1, moved[1], jnp.where(place == 2, moved[2], moved[3])))
        lanes = lanes.astype(bf16)
        high, low = split(dot(jnp.concatenate([lanes, lanes], 1), ty_ref[...]))
        for pg in range(8):
            for part in range(2):
                cut = (slice(pg * 32, (pg + 1) * 32), slice(part * 256, (part + 1) * 256))
                q_ref[c4, pg, part * 32:(part + 1) * 32, :] = high[cut]
                q_ref[c4, pg, 64 + part * 32:64 + (part + 1) * 32, :] = low[cut]

    rows_x(0)
    for c4 in range(4):
        for pg in range(8):
            if pg == 1 and c4 < 3:
                rows_x(c4 + 1)
            q = q_ref[c4, pg]
            field_ref[pg, c4] = dot(tx_ref[...], jnp.concatenate([q, q[:64]], 0)).astype(bf16)
            copies.append(pltpu.make_async_copy(field_ref.at[pg, c4], out_hbm.at[pg, c4], sems.at[c4 * 8 + pg]))
            copies[-1].start()
    for copy in copies:
        copy.wait()


def back(received, terms):
    vmem = pl.BlockSpec(memory_space=pltpu.VMEM)
    anywhere = pl.BlockSpec(memory_space=pl.ANY)
    field, terms = pl.pallas_call(
        back_kernel,
        out_shape=(
            jax.ShapeDtypeStruct((8, 4, NX, NY), bf16),
            jax.ShapeDtypeStruct((2, KZ, 4, C * C), f32),
        ),
        in_specs=[vmem] * 4,
        out_specs=(anywhere, anywhere),
        scratch_shapes=[
            pltpu.VMEM((8, 4, NX, NY), bf16),
            pltpu.VMEM((4, 8, 128, NY), bf16),
            pltpu.SemaphoreType.DMA((33,)),
        ],
        compiler_params=pltpu.CompilerParams(vmem_limit_bytes=VMEM_LIMIT),
        cost_estimate=pl.CostEstimate(flops=4 * 10**9, bytes_accessed=6 * 10**6, transcendentals=0),
        name="back_planes",
    )(received, jnp.asarray(y_back_table()), jnp.asarray(x_back_table()), terms)
    return field.reshape(1, 2, C, NX, NY), terms.transpose(0, 2, 1, 3)


def exchange(chunks, rows):
    moved = lax.all_to_all(chunks.reshape(SLABS, rows, 128), "slab", 0, 0, tiled=True)
    return moved.reshape(SLABS * rows, 128)


def body(field_in, cotangent, weights):
    index = lax.axis_index("group").astype(jnp.int32).reshape(1)
    received = exchange(forward(cotangent, field_in), 16)
    returned = exchange(middle(received, weights), 8)
    pieces = list(input_modes(index, received))
    for k in range(1, 4):
        pieces[k] = lax.ppermute(pieces[k], "group", [(i, i ^ k) for i in range(4)])
    return back(returned, weight_terms(pieces))


def solution(mesh):
    in_specs = (
        P("group", "slab", None, None, None),
        P("group", "slab", None, None, None),
        P(None, "slab", None, None),
    )
    out_specs = (P("group", "slab", None, None, None), P(None, ("slab", "group"), None, None))
    return jax.shard_map(body, mesh=mesh, in_specs=in_specs, out_specs=out_specs, check_vma=False)
```

```python
import math

import jax
import jax.numpy as jnp
import ml_dtypes
import numpy as np
from jax import lax
from jax.experimental import pallas as pl
from jax.experimental.pallas import tpu as pltpu
from jax.sharding import PartitionSpec as P

C = 16
KX = 32
KY = 32
KZ = 17
KP = 24
NX = 256
NY = 256
NZ = 128
SLABS = 64
HALF = KY // 2
SCALE = 1.0 / math.sqrt(NX * NY * NZ)
VMEM_LIMIT = 48 * 1024 * 1024

f32 = jnp.float32
bf16 = jnp.bfloat16


def kept_freqs(keep, length):
    index = np.arange(keep)
    return np.where(index < keep // 2, index, length - keep + index)


def phases(positions, freqs, length):
    turns = positions[:, None] * freqs[None, :] % length
    angle = turns.astype(np.float32) * np.float32(2.0 * math.pi / length)
    return angle.astype(np.float64)


def split_np(table):
    table = np.asarray(table, np.float32)
    high = table.astype(ml_dtypes.bfloat16)
    low = (table - high.astype(np.float32)).astype(ml_dtypes.bfloat16)
    return high, low


def x_forward_table():
    angle = phases(np.arange(NX), kept_freqs(KX, NX), NX)
    high, low = split_np(np.concatenate([np.cos(angle), np.sin(angle)], 1).T)
    return np.concatenate([high, low], 0)


def y_forward_table():
    angle = phases(np.arange(NY), kept_freqs(KY, NY), NY)
    real = np.cos(angle).astype(np.float32).astype(ml_dtypes.bfloat16)
    imag = (-np.sin(angle)).astype(np.float32).astype(ml_dtypes.bfloat16)
    lanes = []
    for half in range(2):
        for part in (real, imag):
            lanes.extend([part[:, half * HALF:(half + 1) * HALF]] * 4)
    return np.concatenate(lanes, 1)


def depth_positions():
    s = np.arange(SLABS)
    return np.concatenate([2 * s, 2 * s + 1])


def depth_forward_table():
    angle = phases(depth_positions(), np.arange(KZ), NZ)
    table = np.zeros((2 * KP, NZ), np.float32)
    table[:KZ] = np.cos(angle).T
    table[KP:KP + KZ] = np.sin(angle).T
    high, low = split_np(table)
    return np.concatenate([high, high, low], 1)


def depth_back_table():
    angle = phases(depth_positions(), np.arange(KZ), NZ)
    table = np.zeros((NZ, 2 * KP), np.float32)
    table[:, :KZ] = np.cos(angle)
    table[:, KP:KP + KZ] = np.sin(angle)
    high, low = split_np(table)
    return np.concatenate([high, high, low], 1)


def channel_mode_lanes():
    lane = np.arange(256)
    return lane // 16, lane % 16


def expand_table():
    c, _ = channel_mode_lanes()
    col = np.arange(256)
    return (c[:, None] == (col % 16)[None]).astype(ml_dtypes.bfloat16)


def collect_table():
    row, col = np.arange(512), np.arange(512)
    channel = col // 128 * 4 + col // 32 % 4
    hit = (row // 256)[:, None] == (col // 16 % 2)[None]
    return (hit & ((row // 16 % 16)[:, None] == channel[None])).astype(ml_dtypes.bfloat16)


def quarter_table():
    c, ky = channel_mode_lanes()
    table = np.zeros((2, 256, 512), np.float32)
    for part in range(2):
        table[part, np.arange(256), ky // 4 * 128 + part * 64 + c * 4 + ky % 4] = 1.0
    return table.reshape(512, 512).astype(ml_dtypes.bfloat16)


def owned_table(which):
    row, col = np.arange(128), np.arange(512)
    target = col // 16 % 16 if which == 0 else col % 16
    hit = (row // 64)[:, None] == (col // 256)[None]
    return (hit & ((row // 4 % 16)[:, None] == target[None])).astype(ml_dtypes.bfloat16)


def y_back_table():
    angle = phases(kept_freqs(KY, NY), np.arange(NY), NY)
    cos, sin = np.cos(angle), np.sin(angle)
    rows = []
    for half in range(2):
        cut = slice(half * HALF, (half + 1) * HALF)
        rows.append(np.concatenate([cos[cut], sin[cut]], 1))
        rows.append(np.concatenate([-sin[cut], cos[cut]], 1))
    high, low = split_np(np.concatenate(rows, 0))
    return np.concatenate([high, high, low, np.zeros_like(low)], 0)


def x_back_table():
    angle = phases(np.arange(NX), kept_freqs(KX, NX), NX)
    table = np.concatenate([np.cos(angle), -np.sin(angle)], 1) * SCALE
    high, low = split_np(table)
    return np.concatenate([high, high, low], 1)


def dot(left, right):
    return jnp.dot(left, right, preferred_element_type=f32)


def split(value):
    high = value.astype(bf16)
    low = (value - high.astype(f32)).astype(bf16)
    return high, low


def lane_iota(rows, lanes):
    return lax.broadcasted_iota(jnp.int32, (rows, lanes), 1)


def swap_parts(value):
    tiles = [pltpu.roll(value[:, t * 128:(t + 1) * 128], 64, 1) for t in range(value.shape[1] // 128)]
    return jnp.concatenate(tiles, 1)


STEPS = 16
WAITS = (2, 3, 4, 7)


def forward_kernel(cot_hbm, fld_hbm, tx_hbm, ty_hbm, out_ref, field_ref, tx_ref, ty_ref, rows_ref, sems):
    tables = [
        pltpu.make_async_copy(ty_hbm, ty_ref, sems.at[STEPS]),
        pltpu.make_async_copy(tx_hbm, tx_ref, sems.at[STEPS + 1]),
    ]
    blocks = []
    for i in range(STEPS):
        source = cot_hbm if i < 8 else fld_hbm
        blocks.append(pltpu.make_async_copy(source.at[pl.ds(i % 8 * 4, 4)], field_ref.at[pl.ds(i * 4, 4)], sems.at[i]))
    for copy in tables + blocks:
        copy.start()
    for copy in tables:
        copy.wait()
    slot = lane_iota(NX, 256) // 16 % 4
    sign = jnp.where(lane_iota(KX, 256) % 128 < 64, 1.0, -1.0)

    def rows_y(i):
        parts = [dot(field_ref[i * 4 + c4], ty_ref[...]) for c4 in range(4)]
        rows = jnp.where(slot == 0, parts[0], jnp.where(slot == 1, parts[1], jnp.where(slot == 2, parts[2], parts[3])))
        high, low = split(rows)
        rows_ref[0, :, i * 256:(i + 1) * 256] = high
        rows_ref[1, :, i * 256:(i + 1) * 256] = low

    def spectra(start, count):
        lanes = slice(start * 256, (start + count) * 256)
        mixed = dot(tx_ref[...], rows_ref[0, :, lanes])
        mixed = mixed[:64] + mixed[64:] + dot(tx_ref[:64], rows_ref[1, :, lanes])
        for j in range(count):
            both = mixed[:, j * 256:(j + 1) * 256]
            result = both[:KX] + sign * swap_parts(both[KX:])
            for half in range(2):
                row = half * 16 + start + j
                out_ref[pl.ds(row, KX, stride=32), :] = result[:, half * 128:(half + 1) * 128]

    first, ready = 0, (0, 0)
    for count in WAITS:
        for i in range(first, first + count):
            blocks[i].wait()
        for i in range(first, first + count):
            rows_y(i)
        if ready[1]:
            spectra(*ready)
        ready = (first, count)
        first += count
    spectra(*ready)


def forward(cotangent, field_in):
    anywhere = pl.BlockSpec(memory_space=pl.ANY)
    return pl.pallas_call(
        forward_kernel,
        out_shape=pltpu.VMEM((SLABS * 16, 128), f32),
        in_specs=[anywhere] * 4,
        scratch_shapes=[
            pltpu.VMEM((STEPS * 4, NX, NY), bf16),
            pltpu.VMEM((128, NX), bf16),
            pltpu.VMEM((NY, 256), bf16),
            pltpu.VMEM((2, NX, STEPS * 256), bf16),
            pltpu.SemaphoreType.DMA((STEPS + 2,)),
        ],
        compiler_params=pltpu.CompilerParams(vmem_limit_bytes=60 * 1024 * 1024),
        cost_estimate=pl.CostEstimate(flops=4 * 10**9, bytes_accessed=9 * 10**6, transcendentals=0),
        name="forward_planes",
    )(
        cotangent.reshape(2 * C, NX, NY),
        field_in.reshape(2 * C, NX, NY),
        jnp.asarray(x_forward_table()),
        jnp.asarray(y_forward_table()),
    )


def roll_half(value):
    return pltpu.roll(value, 64, 1)


def depth_modes(r_ref, first, tz_ref):
    tiles = []
    for cg in range(4):
        rows = [r_ref[pl.ds(first + p * 4 + cg, SLABS, stride=16), :] for p in range(2)]
        tiles.append(jnp.concatenate(rows, 0))
    high, low = split(jnp.concatenate(tiles, 1))
    both = dot(tz_ref[...], jnp.concatenate([high, low, high], 0)) * SCALE
    left = lane_iota(KP, 128) < 64
    real, imag = [], []
    for pair in range(2):
        cuts = [slice((2 * pair + j) * 128, (2 * pair + j + 1) * 128) for j in range(2)]
        c0, c1 = both[:KP, cuts[0]], both[:KP, cuts[1]]
        s0, s1 = both[KP:, cuts[0]], both[KP:, cuts[1]]
        real.append(jnp.where(left, c0 + roll_half(s0), roll_half(c1) + s1))
        imag.append(jnp.where(left, roll_half(c0) - s0, c1 - roll_half(s1)))
    return jnp.concatenate(real, 1), jnp.concatenate(imag, 1)


def precise_dot(value, table):
    high, low = split(value)
    both = dot(jnp.concatenate([high, low], 0), table)
    return both[:value.shape[0]] + both[value.shape[0]:]


def middle_kernel(r_ref, w_ref, tz_ref, e_ref, c_ref, tb_ref, p_ref, g_ref, sum_ref):
    g_real, g_imag = depth_modes(r_ref, 0, tz_ref)
    g_ref[:KP] = g_real
    g_ref[KP:] = g_imag
    own = lane_iota(HALF, 256) % 16 == lax.broadcasted_iota(jnp.int32, (HALF, 256), 0)
    rows = []
    for part in range(2):
        for kz in range(KZ):
            line = g_ref[part * KP + kz:part * KP + kz + 1, :]
            rows.append(jnp.where(own, jnp.broadcast_to(line, (HALF, 256)), 0.0))
    wide = precise_dot(jnp.concatenate(rows, 0), e_ref[...])
    products = []
    for kz in range(KZ):
        g_r = wide[kz * HALF:(kz + 1) * HALF]
        g_i = wide[(KZ + kz) * HALF:(KZ + kz + 1) * HALF]
        w_r, w_i = w_ref[0, kz].astype(f32), w_ref[1, kz].astype(f32)
        products.append(jnp.concatenate([g_r * w_r + g_i * w_i, g_i * w_r - g_r * w_i], 1))
    sums = precise_dot(jnp.concatenate(products, 0), c_ref[...])
    own = jnp.concatenate([own, own], 1)
    sum_ref[...] = jnp.zeros_like(sum_ref)
    for kz in range(KZ):
        kept = jnp.where(own, sums[kz * HALF:(kz + 1) * HALF], 0.0)
        sum_ref[kz:kz + 1, :] = jnp.sum(kept, axis=0, keepdims=True)
    direct = sum_ref[...]
    real_lane = lane_iota(KP, 128) % 32 < 16
    turned = []
    for cg in range(4):
        tile = direct[:, cg * 128:(cg + 1) * 128]
        turned.append(jnp.where(real_lane, -pltpu.roll(tile, 112, 1), pltpu.roll(tile, 16, 1)))
    stacked = jnp.concatenate([direct, jnp.concatenate(turned, 1)], 0)
    high, low = split(stacked)
    planes = dot(tb_ref[...], jnp.concatenate([high, low, high], 0))
    for p in range(2):
        for cg in range(4):
            piece = planes[p * SLABS:(p + 1) * SLABS, cg * 128:(cg + 1) * 128]
            p_ref[pl.ds(p * 4 + cg, SLABS, stride=8), :] = piece


def middle(received, weights):
    return pl.pallas_call(
        middle_kernel,
        out_shape=pltpu.VMEM((SLABS * 8, 128), f32),
        scratch_shapes=[pltpu.VMEM((2 * KP, 256), f32), pltpu.VMEM((KP, 512), f32)],
        compiler_params=pltpu.CompilerParams(vmem_limit_bytes=VMEM_LIMIT),
        cost_estimate=pl.CostEstimate(flops=2 * 10**9, bytes_accessed=3 * 10**6, transcendentals=0),
        name="middle_modes",
    )(
        received,
        weights.transpose(0, 2, 1, 3),
        jnp.asarray(depth_forward_table()),
        jnp.asarray(expand_table()),
        jnp.asarray(collect_table()),
        jnp.asarray(depth_back_table()),
    )


def input_kernel(index_ref, r_ref, tz_ref, cut_ref, own_ref, first_ref, second_ref, third_ref, all_ref):
    u_real, u_imag = depth_modes(r_ref, 8, tz_ref)
    g_real, g_imag = depth_modes(r_ref, 0, tz_ref)
    real = jnp.concatenate([u_real, g_real], 0)
    imag = jnp.concatenate([u_imag, g_imag], 0)
    lanes = precise_dot(real, cut_ref[:256]) + precise_dot(imag, cut_ref[256:])
    for owner in range(4):
        for field in range(2):
            piece = lanes[field * KP:(field + 1) * KP, owner * 128:(owner + 1) * 128]
            all_ref[owner, :, field * 128:(field + 1) * 128] = piece
    me = index_ref[0]
    for k, ref in enumerate((own_ref, first_ref, second_ref, third_ref)):
        ref[...] = all_ref[me ^ k]


def input_modes(index, received):
    vmem = pl.BlockSpec(memory_space=pltpu.VMEM)
    return pl.pallas_call(
        input_kernel,
        out_shape=(jax.ShapeDtypeStruct((KP, 256), f32),) * 4,
        in_specs=[pl.BlockSpec(memory_space=pltpu.SMEM)] + [vmem] * 3,
        out_specs=(vmem,) * 4,
        scratch_shapes=[pltpu.VMEM((4, KP, 256), f32)],
        compiler_params=pltpu.CompilerParams(vmem_limit_bytes=VMEM_LIMIT),
        cost_estimate=pl.CostEstimate(flops=10**8, bytes_accessed=10**6, transcendentals=0),
        name="input_modes",
    )(index, received, jnp.asarray(depth_forward_table()), jnp.asarray(quarter_table()))


def weight_kernel(a_ref, b_ref, c_ref, d_ref, eu_ref, eg_ref, out_ref, u_ref, g_ref):
    mode = lane_iota(KP, 128) % 4
    for k, ref in enumerate((a_ref, b_ref, c_ref, d_ref)):
        for m in range(4):
            rows = pl.ds(k * 4 * KP + m, KP, stride=4)
            u_ref[rows, :] = jnp.where(mode == m, ref[:, :128], 0.0)
            g_ref[rows, :] = jnp.where(mode == m, ref[:, 128:], 0.0)
    u_all = precise_dot(u_ref[...], eu_ref[...])
    g_all = precise_dot(g_ref[...], eg_ref[...])
    real = jnp.zeros((4 * KP, 256), f32)
    imag = jnp.zeros((4 * KP, 256), f32)
    for k in range(4):
        cut = slice(k * 4 * KP, (k + 1) * 4 * KP)
        u_r, u_i = u_all[cut, :256], u_all[cut, 256:]
        g_r, g_i = g_all[cut, :256], g_all[cut, 256:]
        real = real + (u_r * g_r + u_i * g_i)
        imag = imag + (u_r * g_i - u_i * g_r)
    for kz in range(KZ):
        out_ref[0, kz] = real[kz * 4:(kz + 1) * 4]
        out_ref[1, kz] = imag[kz * 4:(kz + 1) * 4]


def weight_terms(pieces):
    return pl.pallas_call(
        weight_kernel,
        out_shape=pltpu.VMEM((2, KZ, 4, C * C), f32),
        scratch_shapes=[pltpu.VMEM((16 * KP, 128), f32), pltpu.VMEM((16 * KP, 128), f32)],
        compiler_params=pltpu.CompilerParams(vmem_limit_bytes=VMEM_LIMIT),
        cost_estimate=pl.CostEstimate(flops=2 * 10**9, bytes_accessed=2 * 10**6, transcendentals=0),
        name="weight_terms",
    )(*pieces, jnp.asarray(owned_table(0)), jnp.asarray(owned_table(1)))


def back_kernel(r_ref, ty_ref, tx_ref, terms_ref, out_hbm, terms_hbm, field_ref, q_ref, sems):
    copies = [pltpu.make_async_copy(terms_ref, terms_hbm, sems.at[32])]
    copies[0].start()
    highs, lows = [], []
    for half in range(2):
        rows = [r_ref[pl.ds(half * 8 + pg, KX, stride=16), :] for pg in range(8)]
        grid = jnp.concatenate(rows, 0)
        highs.append(grid.astype(bf16).astype(f32))
        lows.append(grid - highs[-1])
    parts = highs + lows
    def rows_x(c4, start=0, count=8):
        span = slice(start * 32, (start + count) * 32)
        moved = [parts[t][span] if t == c4 else pltpu.roll(parts[t][span], (t - c4) % 4 * 32, 1) for t in range(4)]
        place = lane_iota(count * 32, 128) // 32
        lanes = jnp.where(place == 0, moved[0], jnp.where(place == 1, moved[1], jnp.where(place == 2, moved[2], moved[3])))
        lanes = lanes.astype(bf16)
        high, low = split(dot(jnp.concatenate([lanes, lanes], 1), ty_ref[...]))
        for pg in range(start, start + count):
            for part in range(2):
                cut = (slice((pg - start) * 32, (pg - start + 1) * 32), slice(part * 256, (part + 1) * 256))
                q_ref[c4, pg, part * 32:(part + 1) * 32, :] = high[cut]
                q_ref[c4, pg, 64 + part * 32:64 + (part + 1) * 32, :] = low[cut]

    rows_x(0, 0, 2)
    for c4 in range(4):
        for pg in range(8):
            if pg == 1 and c4 == 0:
                rows_x(0, 2, 6)
            if pg == 4 and c4 < 3:
                rows_x(c4 + 1)
            q = q_ref[c4, pg]
            field_ref[pg, c4] = dot(tx_ref[...], jnp.concatenate([q, q[:64]], 0)).astype(bf16)
            copies.append(pltpu.make_async_copy(field_ref.at[pg, c4], out_hbm.at[pg, c4], sems.at[c4 * 8 + pg]))
            copies[-1].start()
    for copy in copies:
        copy.wait()


def back(received, terms):
    vmem = pl.BlockSpec(memory_space=pltpu.VMEM)
    anywhere = pl.BlockSpec(memory_space=pl.ANY)
    field, terms = pl.pallas_call(
        back_kernel,
        out_shape=(
            jax.ShapeDtypeStruct((8, 4, NX, NY), bf16),
            jax.ShapeDtypeStruct((2, KZ, 4, C * C), f32),
        ),
        in_specs=[vmem] * 4,
        out_specs=(anywhere, anywhere),
        scratch_shapes=[
            pltpu.VMEM((8, 4, NX, NY), bf16),
            pltpu.VMEM((4, 8, 128, NY), bf16),
            pltpu.SemaphoreType.DMA((33,)),
        ],
        compiler_params=pltpu.CompilerParams(vmem_limit_bytes=VMEM_LIMIT),
        cost_estimate=pl.CostEstimate(flops=4 * 10**9, bytes_accessed=6 * 10**6, transcendentals=0),
        name="back_planes",
    )(received, jnp.asarray(y_back_table()), jnp.asarray(x_back_table()), terms)
    return field.reshape(1, 2, C, NX, NY), terms.transpose(0, 2, 1, 3)


def exchange(chunks, rows):
    moved = lax.all_to_all(chunks.reshape(SLABS, rows, 128), "slab", 0, 0, tiled=True)
    return moved.reshape(SLABS * rows, 128)


def body(field_in, cotangent, weights):
    index = lax.axis_index("group").astype(jnp.int32).reshape(1)
    received = exchange(forward(cotangent, field_in), 16)
    returned = exchange(middle(received, weights), 8)
    pieces = list(input_modes(index, received))
    for k in range(1, 4):
        pieces[k] = lax.ppermute(pieces[k], "group", [(i, i ^ k) for i in range(4)])
    return back(returned, weight_terms(pieces))


def solution(mesh):
    in_specs = (
        P("group", "slab", None, None, None),
        P("group", "slab", None, None, None),
        P(None, "slab", None, None),
    )
    out_specs = (P("group", "slab", None, None, None), P(None, ("slab", "group"), None, None))
    return jax.shard_map(body, mesh=mesh, in_specs=in_specs, out_specs=out_specs, check_vma=False)
```
